128 devices in a mesh: dp: 8 (over x, core), group: 16 (over z, y).
Axes of the slice: x: 4, y: 4, z: 4, core: 2. Of those that a mesh axis runs over, the one named last changes fastest.
Arguments:
- query_first: bfloat16 [131072, 256], P(('dp', 'group')), may hold values from -400 to 400
- query_second: bfloat16 [131072, 512], P(('dp', 'group')), may hold values from -400 to 400
- query_third: bfloat16 [131072, 1024], P(('dp', 'group')), may hold values from -400 to 400
- passage_first: bfloat16 [131072, 256], P(('dp', 'group')), may hold values from -400 to 400
- passage_second: bfloat16 [131072, 512], P(('dp', 'group')), may hold values from -400 to 400
- passage_third: bfloat16 [131072, 1024], P(('dp', 'group')), may hold values from -400 to 400
- neg_blocks: int32 [512, 127], P(('dp', 'group')), may hold values from -1 to 16383, as said below
- positives: int32 [131072], P(('dp', 'group')), may hold values from 0 to 131071, as said below
Outputs:
- losses: float32 [131072], P(('dp', 'group'))
- grad_query_first: float32 [131072, 256], P(('dp', 'group'))
- grad_query_second: float32 [131072, 512], P(('dp', 'group'))
- grad_query_third: float32 [131072, 1024], P(('dp', 'group'))
- grad_passage_first: float32 [131072, 256], P(('dp', 'group'))
- grad_passage_second: float32 [131072, 512], P(('dp', 'group'))
- grad_passage_third: float32 [131072, 1024], P(('dp', 'group'))
The draws below stay inside these ranges and needn't reach their ends.
Inputs may be any that keep to these rules, and one draw needn't show every extreme that they name: `neg_blocks`: row b lists hard-negative blocks of query block b (queries b * 256 to (b + 1) * 256 - 1). Block k is the passage rows k * 8 to (k + 1) * 8 - 1 and lies on device k // 128 in the order of dp+group. A row holds a quarter of 127 (rounded down) to 127 distinct block ids first and -1 after them; some row holds 127. No row names a block of its own query block's device. Over all rows of one device, the named blocks that lie on any one other device are one and the same block. `positives`: the positive of a query is a passage row of the query's own device; every passage row is the positive of exactly one query.
All inputs are finite; a program needn't handle non-finite values.
Results may differ from the reference program's by a relative error of at most 0.0041.
Values may be sent and summed in bfloat16 or wider, within the bound.
No kernel may reach another device: no remote copies, remote signals or barrier semaphores. Data moves between devices by JAX's collectives and lax.ppermute only.
A program may use at most 128 MiB of HBM per device.

```python
import math
import jax
import jax.numpy as jnp
from jax import lax

W1 = 256
W2 = 512
W3 = 1024
BLK_Q = 256
PROWS = 8
QB_DEV = 4
PBLK_DEV = 128
NQ = 131072
NQB = 512
LISTMAX = 127
DEVICES = 128


def scaled(key, base):
    key_rows, key_cols = jax.random.split(key)
    row_scale = jnp.exp(jax.random.uniform(key_rows, (base.shape[0], 1), jnp.float32, 0.0, math.log(10.0)))
    col_scale = jnp.exp(jax.random.uniform(key_cols, (1, base.shape[1]), jnp.float32, 0.0, math.log(10.0)))
    return (jnp.clip(base, -4.0, 4.0) * row_scale * col_scale).astype(jnp.bfloat16)


def draw_query_first(key, part):
    key = jax.random.fold_in(key, 1)
    key_base, key_scale = jax.random.split(key, 2)
    base = jax.random.normal(key_base, (NQ, W1), jnp.float32)
    return scaled(key_scale, base)


def draw_query_second(key, part):
    key = jax.random.fold_in(key, 2)
    key_base, key_scale = jax.random.split(key, 2)
    base = jax.random.normal(key_base, (NQ, W2), jnp.float32)
    return scaled(key_scale, base)


def draw_query_third(key, part):
    key = jax.random.fold_in(key, 3)
    key_base, key_scale = jax.random.split(key, 2)
    base = jax.random.normal(key_base, (NQ, W3), jnp.float32)
    return scaled(key_scale, base)


def draw_passage_first(key, part):
    key = jax.random.fold_in(key, 4)
    key_base, key_scale = jax.random.split(key, 2)
    base = jax.random.normal(key_base, (NQ, W1), jnp.float32)
    return scaled(key_scale, base)


def draw_passage_second(key, part):
    key = jax.random.fold_in(key, 5)
    key_base, key_scale = jax.random.split(key, 2)
    base = jax.random.normal(key_base, (NQ, W2), jnp.float32)
    return scaled(key_scale, base)


def draw_passage_third(key, part):
    key = jax.random.fold_in(key, 6)
    key_base, key_scale = jax.random.split(key, 2)
    base = jax.random.normal(key_base, (NQ, W3), jnp.float32)
    return scaled(key_scale, base)


def shuffle_peers(subkey):
    return jax.random.permutation(subkey, LISTMAX)


def shuffle_rows(subkey):
    return jax.random.permutation(subkey, QB_DEV * BLK_Q)


def draw_neg_blocks(key, part):
    key = jax.random.fold_in(key, 11)
    key_chosen, key_counts, key_forced, key_order = jax.random.split(key, 4)
    chosen = jax.random.randint(key_chosen, (DEVICES, DEVICES), 0, PBLK_DEV)
    counts = jax.random.randint(key_counts, (NQB,), max(1, LISTMAX // 4), LISTMAX + 1)
    forced = jax.random.randint(key_forced, (), 0, NQB)
    counts = jnp.where(jnp.arange(NQB) == forced, LISTMAX, counts)
    orders = jax.vmap(shuffle_peers)(jax.random.split(key_order, NQB))
    requester = (jnp.arange(NQB) // QB_DEV)[:, None]
    peers = orders + (orders >= requester).astype(jnp.int32)
    local_ids = chosen[requester, peers]
    block_ids = peers * PBLK_DEV + local_ids
    entries = jnp.arange(LISTMAX)[None, :]
    return jnp.where(entries < counts[:, None], block_ids, -1).astype(jnp.int32)


def draw_positives(key, part):
    key = jax.random.fold_in(key, 7)
    orders = jax.vmap(shuffle_rows)(jax.random.split(key, DEVICES))
    starts = jnp.arange(DEVICES)[:, None] * (QB_DEV * BLK_Q)
    return (orders + starts).reshape(NQ).astype(jnp.int32)


def setup_inputs(seed: int = 0) -> dict:
    key_list = jax.random.split(jax.random.key(seed), 9)
    return {
        "query_first": draw_query_first(jax.random.fold_in(key_list[8], 71), 0),
        "query_second": draw_query_second(jax.random.fold_in(key_list[8], 71), 0),
        "query_third": draw_query_third(jax.random.fold_in(key_list[8], 71), 0),
        "passage_first": draw_passage_first(jax.random.fold_in(key_list[8], 71), 0),
        "passage_second": draw_passage_second(jax.random.fold_in(key_list[8], 71), 0),
        "passage_third": draw_passage_third(jax.random.fold_in(key_list[8], 71), 0),
        "neg_blocks": draw_neg_blocks(jax.random.fold_in(key_list[8], 71), 0),
        "positives": draw_positives(jax.random.fold_in(key_list[8], 71), 0),
    }


epsilon = 1e-06
sharpness = 20.0

def unit_rows(values):
    widened = values.astype(jnp.float32)
    inverse = lax.rsqrt(lax.optimization_barrier(jnp.sum(widened * widened, axis=1, keepdims=True)) + epsilon)
    return (widened * inverse, inverse)

def raw_gradient(unit, inverse, head_grad):
    return (head_grad - unit * lax.optimization_barrier(jnp.sum(unit * head_grad, axis=1, keepdims=True))) * inverse

def exit_step(query_raw, passage_raw, neg_blocks, positives):
    query_rows = QB_DEV * BLK_Q
    width = query_raw.shape[1]
    offsets = jnp.arange(PROWS, dtype=jnp.int32)
    q_unit, q_inverse = unit_rows(query_raw)
    p_unit, p_inverse = unit_rows(passage_raw)
    q_head = q_unit.astype(jnp.bfloat16)
    p_head = p_unit.astype(jnp.bfloat16)

    def device_step(carry, device):
        start = (device * query_rows).astype(jnp.int32)
        q_device = lax.dynamic_slice_in_dim(q_head, start, query_rows, 0)
        p_device = lax.dynamic_slice_in_dim(p_head, start, query_rows, 0)
        local_pos = lax.dynamic_slice_in_dim(positives, start, query_rows, 0) - start
        block_lists = lax.dynamic_slice_in_dim(neg_blocks, (device * QB_DEV).astype(jnp.int32), QB_DEV, 0)
        present = block_lists >= 0
        far_rows = (jnp.maximum(block_lists, 0)[:, :, None] * PROWS + offsets[None, None, :]).reshape(QB_DEV, LISTMAX * PROWS)
        far_weight = jnp.repeat(present, PROWS, axis=1).astype(jnp.float32)
        far_heads = p_head[far_rows]
        q_blocks = q_device.reshape(QB_DEV, BLK_Q, width)
        s_local = sharpness * jnp.dot(q_device, p_device.T, preferred_element_type=jnp.float32)
        s_far = sharpness * jnp.einsum('bqw,bjw->bqj', q_blocks.astype(jnp.float32), far_heads.astype(jnp.float32))
        e_local = jnp.exp(s_local)
        e_far = jnp.exp(s_far) * far_weight[:, None, :]
        totals = lax.optimization_barrier(jnp.sum(e_local, axis=1, keepdims=True)) + lax.optimization_barrier(jnp.sum(e_far, axis=2)).reshape(query_rows, 1)
        onehot = (jnp.arange(query_rows, dtype=jnp.int32)[None, :] == local_pos[:, None]).astype(jnp.float32)
        loss_device = jnp.log(totals[:, 0]) - lax.optimization_barrier(jnp.sum(s_local * onehot, axis=1))
        g_local = (sharpness * (e_local / totals - onehot)).astype(jnp.bfloat16)
        g_far = (sharpness * (e_far / totals.reshape(QB_DEV, BLK_Q, 1))).astype(jnp.bfloat16)
        q_grad = jnp.dot(g_local, p_device, preferred_element_type=jnp.float32) + jnp.einsum('bqj,bjw->bqw', g_far.astype(jnp.float32), far_heads.astype(jnp.float32)).reshape(query_rows, width)
        local_grad = jnp.dot(g_local.T, q_device, preferred_element_type=jnp.float32)
        far_grad = jnp.einsum('bqj,bqw->bjw', g_far.astype(jnp.float32), q_blocks.astype(jnp.float32)).reshape(QB_DEV * LISTMAX * PROWS, width)
        current = lax.dynamic_slice_in_dim(carry, start, query_rows, 0)
        carry = lax.dynamic_update_slice_in_dim(carry, current + local_grad, start, 0)
        carry = carry.at[far_rows.reshape(-1)].add(far_grad)
        return (carry, (loss_device, q_grad))
    p_total, (loss_parts, q_parts) = lax.scan(device_step, jnp.zeros((NQ, width), jnp.float32), jnp.arange(DEVICES, dtype=jnp.int32))
    q_out = raw_gradient(q_unit, q_inverse, q_parts.reshape(NQ, width))
    p_out = raw_gradient(p_unit, p_inverse, p_total)
    return (loss_parts.reshape(NQ), q_out, p_out)

def reference(query_first, query_second, query_third, passage_first, passage_second, passage_third, neg_blocks, positives):
    loss_first, q_first, p_first = exit_step(query_first, passage_first, neg_blocks, positives)
    loss_second, q_second, p_second = exit_step(query_second, passage_second, neg_blocks, positives)
    loss_third, q_third, p_third = exit_step(query_third, passage_third, neg_blocks, positives)
    losses = loss_first + loss_second + loss_third
    return (losses, q_first, q_second, q_third, p_first, p_second, p_third)
```

```python
import functools
import math

import jax
import jax.numpy as jnp
from jax import lax
from jax.experimental import pallas as pl
from jax.experimental.pallas import tpu as pltpu
from jax.sharding import PartitionSpec as P

PROWS = 8
LANES = 128
AXES = ("dp", "group")

EPSILON = 1e-06
SHARPNESS = 20.0
EXP_SCALE = SHARPNESS * math.log2(math.e)
OFF = -1e30

F32 = jnp.float32
BF16 = jnp.bfloat16
ANY = pl.BlockSpec(memory_space=pl.ANY)
VMEM = pl.BlockSpec(memory_space=pltpu.VMEM)
SMEM = pl.BlockSpec(memory_space=pltpu.SMEM)
MIB = 1024 * 1024
NT = (((1,), (1,)), ((), ()))
TN = (((0,), (0,)), ((), ()))
NN = (((1,), (0,)), ((), ()))


def exchange(values):
    return lax.all_to_all(values, AXES, split_axis=0, concat_axis=0, tiled=True)


def cost(flops, moved):
    return pl.CostEstimate(flops=int(flops), bytes_accessed=int(moved), transcendentals=0)


def columns_of(widths):
    starts = {}
    at = 0
    for index in sorted(range(len(widths)), key=lambda i: -widths[i]):
        starts[index] = at
        at += widths[index]
    return [starts[i] for i in range(len(widths))]


def wanted_kernel(block_count, neg_ref, out_ref):
    peers = out_ref.shape[0]
    lists, entries = neg_ref.shape
    peer = lax.broadcasted_iota(jnp.int32, (peers, entries), 0)
    best = jnp.full((peers, 1), -1, jnp.int32)
    for row in range(lists):
        ids = jnp.broadcast_to(neg_ref[row : row + 1, :], (peers, entries))
        local_ids = ids - peer * block_count
        hit = (local_ids >= 0) & (local_ids < block_count)
        best = jnp.maximum(best, jnp.max(jnp.where(hit, local_ids, -1), axis=1, keepdims=True))
    out_ref[...] = jnp.broadcast_to(best, out_ref.shape)


def heads_kernel(widths, starts, *refs):
    raws, (q_out, p_out, inv_out) = refs[:6], refs[6:]
    lane = lax.broadcasted_iota(jnp.int32, inv_out.shape, 1)
    packed = jnp.zeros(inv_out.shape, F32)
    for side, out in enumerate((q_out, p_out)):
        for k in range(3):
            values = raws[side * 3 + k][...].astype(F32)
            inverse = lax.rsqrt(jnp.sum(values * values, axis=1, keepdims=True) + EPSILON)
            out[:, starts[k] : starts[k] + widths[k]] = (values * inverse).astype(BF16)
            packed = jnp.where(lane == side * 3 + k, inverse, packed)
    inv_out[...] = packed


def gather_kernel(pairs, asked_ref, p_ref, out_ref):
    base = pl.program_id(0) * pairs

    def block(peer):
        ident = jnp.maximum(asked_ref[peer, 0], 0)
        start = pl.multiple_of((ident // 2) * 16, 16)
        both = p_ref[pl.ds(start, 16), :].astype(F32)
        return jnp.where(ident % 2 == 0, both[:8], both[8:])

    for pair in range(pairs):
        peer = (base + pair) * 2
        rows = jnp.concatenate([block(peer), block(peer + 1)], axis=0)
        out_ref[pair * 16 : pair * 16 + 16, :] = rows.astype(BF16)


def local_kernel(widths, starts, block_count, p_ref, q_ref, pos_ref, neg_ref, tot_ref, spos_ref, bias_ref):
    rows = p_ref.shape[0]
    cols = q_ref.shape[0]
    chunk = min(256, rows)
    pos = pos_ref[0:1, :]
    for k in range(3):
        span = slice(starts[k], starts[k] + widths[k])
        q = q_ref[:, span]
        tot = jnp.zeros((1, cols), F32)
        spos = jnp.zeros((1, cols), F32)
        for at in range(0, rows, chunk):
            s = lax.dot_general(p_ref[at : at + chunk, span], q, NT, preferred_element_type=F32)
            row = lax.broadcasted_iota(jnp.int32, (chunk, cols), 0) + at
            tot = tot + jnp.sum(jnp.exp2(s * EXP_SCALE), axis=0, keepdims=True)
            spos = spos + jnp.sum(jnp.where(row == pos, s, 0.0), axis=0, keepdims=True)
        tot_ref[k : k + 1, :] = tot
        spos_ref[k : k + 1, :] = spos * SHARPNESS
    far = bias_ref.shape[0]
    entries = neg_ref.shape[2]
    peer = lax.broadcasted_iota(jnp.int32, (far, entries), 0) // PROWS
    local_ids = jnp.broadcast_to(neg_ref[0], (far, entries)) - peer * block_count
    hit = (local_ids >= 0) & (local_ids < block_count)
    listed = jnp.max(jnp.where(hit, 1.0, 0.0), axis=1, keepdims=True)
    bias_ref[...] = jnp.broadcast_to(jnp.where(listed > 0.0, 0.0, OFF), bias_ref.shape)


def far_kernel(
    widths, starts, lists, far_any, q_any, bias_ref, tot_ref, spos_ref,
    term_any, g_any, scale_ref, loss_ref,
    far_v, q_v, e_v, g_v, term_v, in_sems, g_sems, term_sems,
):
    far, rows = g_v.shape[1], g_v.shape[2]
    cols = rows // lists
    chunk = min(256, far)
    order = (0, 1, 2)
    loads = {}
    for k in order:
        span = pl.ds(starts[k], widths[k])
        loads[k] = (
            pltpu.make_async_copy(far_any.at[:, span], far_v.at[:, span], in_sems.at[k, 0]),
            pltpu.make_async_copy(q_any.at[:, span], q_v.at[:, span], in_sems.at[k, 1]),
        )
        for load in loads[k]:
            load.start()
    stores = []
    loss = jnp.zeros((1, rows), F32)
    for k in order:
        span = slice(starts[k], starts[k] + widths[k])
        for load in loads[k]:
            load.wait()
        for b in range(lists):
            at_q = slice(b * cols, (b + 1) * cols)
            q = q_v[at_q, span]
            tot = tot_ref[k : k + 1, at_q]
            for at in range(0, far, chunk):
                s = lax.dot_general(far_v[at : at + chunk, span], q, NT, preferred_element_type=F32)
                bias = bias_ref[at : at + chunk, b * LANES : b * LANES + 1]
                e = jnp.exp2(s * EXP_SCALE + bias)
                tot = tot + jnp.sum(e, axis=0, keepdims=True)
                e_v[at : at + chunk, at_q] = e
            scale = SHARPNESS / tot
            scale_ref[k : k + 1, at_q] = scale
            loss_ref[k : k + 1, at_q] = jnp.log(tot) - spos_ref[k : k + 1, at_q]
            for at in range(0, far, chunk):
                g_v[k, at : at + chunk, at_q] = (e_v[at : at + chunk, at_q] * scale).astype(BF16)
        store = pltpu.make_async_copy(g_v.at[k], g_any.at[k], g_sems.at[k])
        store.start()
        stores.append(store)
        step = 256
        for at in range(0, widths[k], step):
            here = slice(starts[k] + at, starts[k] + at + step)
            for row in range(0, far, chunk):
                part = jnp.dot(g_v[k, row : row + chunk, :], q_v[:, here], preferred_element_type=F32)
                term_v[row : row + chunk, here] = part.astype(BF16)
        store = pltpu.make_async_copy(
            term_v.at[:, pl.ds(starts[k], widths[k])],
            term_any.at[:, pl.ds(starts[k], widths[k])],
            term_sems.at[k],
        )
        store.start()
        stores.append(store)
    for store in stores:
        store.wait()


def near_kernel(
    k, p_ref, q_ref, far_ref, g_ref, raw_ref, inv_ref, scale_ref, pos_ref, out_ref, dp_ref
):
    rows = p_ref.shape[0]
    cols = q_ref.shape[0]
    q = q_ref[...]
    pos = pos_ref[0:1, :]
    scale = scale_ref[k : k + 1, :]
    chunk = min(256, rows)
    first = pl.program_id(0) == 0
    dq = lax.dot_general(g_ref[0], far_ref[...], TN, preferred_element_type=F32)
    parts = []
    for at in range(0, rows, chunk):
        s = lax.dot_general(p_ref[at : at + chunk, :], q, NT, preferred_element_type=F32)
        row = lax.broadcasted_iota(jnp.int32, (chunk, cols), 0) + at
        g = jnp.exp2(s * EXP_SCALE) * scale
        parts.append((g - jnp.where(row == pos, SHARPNESS, 0.0)).astype(BF16))
    weights = jnp.concatenate(parts, axis=0)
    dq = dq + lax.dot_general(weights, p_ref[...], TN, preferred_element_type=F32)
    dp = jnp.dot(weights, q, preferred_element_type=F32)

    @pl.when(first)
    def _():
        dp_ref[...] = dp

    @pl.when(jnp.logical_not(first))
    def _():
        dp_ref[...] += dp

    inverse = inv_ref[:, k : k + 1]
    unit = raw_ref[...].astype(F32) * inverse
    out_ref[...] = (dq - unit * jnp.sum(unit * dq, axis=1, keepdims=True)) * inverse


def passage_kernel(
    widths, starts, asked_ref, term_any, dp0, dp1, dp2, raw0, raw1, raw2, inv_ref,
    out0, out1, out2,
    term_v, acc0, acc1, acc2, rv0, rv1, rv2, in_sems, out_sems,
):
    dps, raws, outs = (dp0, dp1, dp2), (raw0, raw1, raw2), (out0, out1, out2)
    accs, raw_vs = (acc0, acc1, acc2), (rv0, rv1, rv2)
    rows = acc0.shape[0]
    peers = term_v.shape[0] // PROWS
    order = (0, 1, 2)
    loads = {}
    for k in order:
        span = pl.ds(starts[k], widths[k])
        loads[k] = (
            pltpu.make_async_copy(term_any.at[:, span], term_v.at[:, span], in_sems.at[k, 0]),
            pltpu.make_async_copy(dps[k], accs[k], in_sems.at[k, 1]),
            pltpu.make_async_copy(raws[k], raw_vs[k], in_sems.at[k, 2]),
        )
        for load in loads[k]:
            load.start()
    stores = []
    chunk = rows // 4
    for k in order:
        for load in loads[k]:
            load.wait()
        acc, raw = accs[k], raw_vs[k]
        span = pl.ds(starts[k], widths[k])

        def add(pair, carry):
            both = term_v[pl.ds(pl.multiple_of(pair * 16, 16), 16), span].astype(F32)
            for half in range(2):
                ident = jnp.maximum(asked_ref[pair * 2 + half, 0], 0)
                place = pl.ds(pl.multiple_of(ident * PROWS, PROWS), PROWS)
                acc[place, :] = acc[place, :] + both[half * 8 : half * 8 + 8]
            return carry

        lax.fori_loop(0, peers // 2, add, 0)
        for c in range(4):
            def finish(step, carry):
                place = pl.ds(pl.multiple_of(c * chunk + step * 32, 32), 32)
                inverse = inv_ref[place, 3 + k : 4 + k]
                unit = raw[place, :].astype(F32) * inverse
                dp = acc[place, :]
                dot = jnp.sum(unit * dp, axis=1, keepdims=True)
                acc[place, :] = (dp - unit * dot) * inverse
                return carry

            lax.fori_loop(0, chunk // 32, finish, 0)
            part = pl.ds(c * chunk, chunk)
            store = pltpu.make_async_copy(acc.at[part, :], outs[k].at[part, :], out_sems.at[k, c])
            store.start()
            stores.append(store)
    for store in stores:
        store.wait()


def local(
    query_first, query_second, query_third,
    passage_first, passage_second, passage_third,
    neg_blocks, positives,
):
    devices = lax.axis_size(AXES)
    own = lax.axis_index(AXES)
    queries = (query_first, query_second, query_third)
    passages = (passage_first, passage_second, passage_third)
    widths = [values.shape[1] for values in queries]
    starts = columns_of(widths)
    wide = sum(widths)
    rows = query_first.shape[0]
    block_count = rows // PROWS
    lists, entries = neg_blocks.shape
    far = devices * PROWS
    cols = rows // lists
    params = functools.partial(pltpu.CompilerParams)

    wanted = pl.pallas_call(
        functools.partial(wanted_kernel, block_count),
        out_shape=jax.ShapeDtypeStruct((devices, LANES), jnp.int32),
        in_specs=[VMEM],
        out_specs=VMEM,
    )(neg_blocks)
    asked = exchange(wanted[:, None, :]).reshape(devices, LANES)

    step = rows // 8
    row_block = lambda width: pl.BlockSpec((step, width), lambda i: (i, 0))
    q_all, p_all, inverses = pl.pallas_call(
        functools.partial(heads_kernel, widths, starts),
        grid=(8,),
        out_shape=(
            jax.ShapeDtypeStruct((rows, wide), BF16),
            jax.ShapeDtypeStruct((rows, wide), BF16),
            jax.ShapeDtypeStruct((rows, LANES), F32),
        ),
        in_specs=[row_block(width) for width in widths + widths],
        out_specs=(row_block(wide), row_block(wide), row_block(LANES)),
        compiler_params=params(vmem_limit_bytes=24 * MIB),
        cost_estimate=cost(rows * wide * 8, rows * wide * 8),
    )(*queries, *passages)

    pairs = max(1, devices // 2 // 8)
    send = pl.pallas_call(
        functools.partial(gather_kernel, pairs),
        grid=(devices // 2 // pairs,),
        out_shape=jax.ShapeDtypeStruct((far, wide), BF16),
        in_specs=[SMEM, pl.BlockSpec((rows, wide), lambda i: (0, 0))],
        out_specs=pl.BlockSpec((pairs * 16, wide), lambda i: (i, 0)),
        compiler_params=params(vmem_limit_bytes=24 * MIB),
        cost_estimate=cost(far * wide, far * wide * 4),
    )(asked, p_all)
    fetched = exchange(send.reshape(devices, PROWS, wide)).reshape(far, wide)

    local_pos = (positives - own * rows).reshape(1, rows)
    whole = lambda shape: pl.BlockSpec(shape, lambda i: (0,) * len(shape))
    lane_block = pl.BlockSpec((8, cols), lambda i: (0, i))
    pos_block = pl.BlockSpec((1, cols), lambda i: (0, i))
    totals, positive_scores, bias = pl.pallas_call(
        functools.partial(local_kernel, widths, starts, block_count),
        grid=(lists,),
        out_shape=(
            jax.ShapeDtypeStruct((8, rows), F32),
            jax.ShapeDtypeStruct((8, rows), F32),
            jax.ShapeDtypeStruct((far, lists * LANES), F32),
        ),
        in_specs=[
            whole((rows, wide)),
            pl.BlockSpec((cols, wide), lambda i: (i, 0)),
            pos_block,
            pl.BlockSpec((1, 1, entries), lambda i: (i, 0, 0)),
        ],
        out_specs=(lane_block, lane_block, pl.BlockSpec((far, LANES), lambda i: (0, i))),
        compiler_params=params(vmem_limit_bytes=32 * MIB),
        cost_estimate=cost(2 * rows * rows * wide, rows * wide * 4),
    )(p_all, q_all, local_pos, neg_blocks.reshape(lists, 1, entries))

    terms, far_weights, scales, loss_rows = pl.pallas_call(
        functools.partial(far_kernel, widths, starts, lists),
        out_shape=(
            jax.ShapeDtypeStruct((far, wide), BF16),
            jax.ShapeDtypeStruct((3, far, rows), BF16),
            jax.ShapeDtypeStruct((8, rows), F32),
            jax.ShapeDtypeStruct((8, rows), F32),
        ),
        in_specs=[ANY, ANY, VMEM, VMEM, VMEM],
        out_specs=(ANY, ANY, VMEM, VMEM),
        scratch_shapes=[
            pltpu.VMEM((far, wide), BF16),
            pltpu.VMEM((rows, wide), BF16),
            pltpu.VMEM((far, rows), F32),
            pltpu.VMEM((3, far, rows), BF16),
            pltpu.VMEM((far, wide), BF16),
            pltpu.SemaphoreType.DMA((3, 2)),
            pltpu.SemaphoreType.DMA((3,)),
            pltpu.SemaphoreType.DMA((3,)),
        ],
        compiler_params=params(vmem_limit_bytes=40 * MIB),
        cost_estimate=cost(4 * far * rows * wide, 6 * far * wide),
    )(fetched, q_all, bias, totals, positive_scores)
    losses = loss_rows[0] + loss_rows[1] + loss_rows[2]
    returned = exchange(terms.reshape(devices, PROWS, wide)).reshape(far, wide)

    q_grads = []
    dp_parts = []
    for k in range(3):
        width = widths[k]
        place = starts[k] // width
        q_grad, dp_part = pl.pallas_call(
            functools.partial(near_kernel, k),
            grid=(lists,),
            out_shape=(
                jax.ShapeDtypeStruct((rows, width), F32),
                jax.ShapeDtypeStruct((rows, width), F32),
            ),
            in_specs=[
                pl.BlockSpec((rows, width), lambda i, place=place: (0, place)),
                pl.BlockSpec((cols, width), lambda i, place=place: (i, place)),
                pl.BlockSpec((far, width), lambda i, place=place: (0, place)),
                pl.BlockSpec((1, far, cols), lambda i, k=k: (k, 0, i)),
                pl.BlockSpec((cols, width), lambda i: (i, 0)),
                pl.BlockSpec((cols, LANES), lambda i: (i, 0)),
                lane_block,
                pos_block,
            ],
            out_specs=(
                pl.BlockSpec((cols, width), lambda i: (i, 0)),
                pl.BlockSpec((rows, width), lambda i: (0, 0)),
            ),
            compiler_params=params(vmem_limit_bytes=40 * MIB),
            cost_estimate=cost(8 * rows * rows * width, 16 * rows * width),
        )(p_all, q_all, fetched, far_weights, queries[k], inverses, scales, local_pos)
        q_grads.append(q_grad)
        dp_parts.append(dp_part)

    p_grads = pl.pallas_call(
        functools.partial(passage_kernel, widths, starts),
        out_shape=tuple(jax.ShapeDtypeStruct((rows, width), F32) for width in widths),
        in_specs=[SMEM] + [ANY] * 7 + [VMEM],
        out_specs=(ANY, ANY, ANY),
        scratch_shapes=[pltpu.VMEM((far, wide), BF16)]
        + [pltpu.VMEM((rows, width), F32) for width in widths]
        + [pltpu.VMEM((rows, width), BF16) for width in widths]
        + [pltpu.SemaphoreType.DMA((3, 3)), pltpu.SemaphoreType.DMA((3, 4))],
        compiler_params=params(vmem_limit_bytes=32 * MIB),
        cost_estimate=cost(16 * rows * wide, 12 * rows * wide),
    )(asked, returned, *dp_parts, *passages, inverses)
    return (losses, *q_grads, *p_grads)


def solution(mesh):
    rows = P(AXES, None)
    return jax.shard_map(
        local,
        mesh=mesh,
        in_specs=(rows,) * 7 + (P(AXES),),
        out_specs=(P(AXES),) + (rows,) * 6,
        check_vma=False,
    )
```

```python
import functools
import math

import jax
import jax.numpy as jnp
from jax import lax
from jax.experimental import pallas as pl
from jax.experimental.pallas import tpu as pltpu
from jax.sharding import PartitionSpec as P

PROWS = 8
LANES = 128
AXES = ("dp", "group")

EPSILON = 1e-06
SHARPNESS = 20.0
EXP_SCALE = SHARPNESS * math.log2(math.e)
OFF = -1e30

F32 = jnp.float32
BF16 = jnp.bfloat16
HBM = pl.BlockSpec(memory_space=pltpu.HBM)
VMEM = pl.BlockSpec(memory_space=pltpu.VMEM)
SMEM = pl.BlockSpec(memory_space=pltpu.SMEM)
MIB = 1024 * 1024
NT = (((1,), (1,)), ((), ()))
TN = (((0,), (0,)), ((), ()))
NN = (((1,), (0,)), ((), ()))


def exchange(values):
    return lax.all_to_all(values, AXES, split_axis=0, concat_axis=0, tiled=True)


def cost(flops, moved):
    return pl.CostEstimate(flops=int(flops), bytes_accessed=int(moved), transcendentals=0)


def columns_of(widths):
    starts = {}
    at = 0
    for index in sorted(range(len(widths)), key=lambda i: -widths[i]):
        starts[index] = at
        at += widths[index]
    return [starts[i] for i in range(len(widths))]


def wanted_kernel(block_count, neg_ref, out_ref):
    peers = out_ref.shape[0]
    lists, entries = neg_ref.shape
    peer = lax.broadcasted_iota(jnp.int32, (peers, entries), 0)
    best = jnp.full((peers, 1), -1, jnp.int32)
    for row in range(lists):
        ids = jnp.broadcast_to(neg_ref[row : row + 1, :], (peers, entries))
        local_ids = ids - peer * block_count
        hit = (local_ids >= 0) & (local_ids < block_count)
        best = jnp.maximum(best, jnp.max(jnp.where(hit, local_ids, -1), axis=1, keepdims=True))
    out_ref[...] = jnp.broadcast_to(best, out_ref.shape)


def heads_kernel(widths, starts, *refs):
    raws, (q_out, p_out, inv_out) = refs[:6], refs[6:]
    lane = lax.broadcasted_iota(jnp.int32, inv_out.shape, 1)
    packed = jnp.zeros(inv_out.shape, F32)
    for side, out in enumerate((q_out, p_out)):
        for k in range(3):
            values = raws[side * 3 + k][...].astype(F32)
            inverse = lax.rsqrt(jnp.sum(values * values, axis=1, keepdims=True) + EPSILON)
            out[:, starts[k] : starts[k] + widths[k]] = (values * inverse).astype(BF16)
            packed = jnp.where(lane == side * 3 + k, inverse, packed)
    inv_out[...] = packed


def gather_kernel(pairs, asked_ref, p_ref, out_ref):
    base = pl.program_id(0) * pairs

    def block(peer):
        ident = jnp.maximum(asked_ref[peer, 0], 0)
        start = pl.multiple_of((ident // 2) * 16, 16)
        both = p_ref[pl.ds(start, 16), :].astype(F32)
        return jnp.where(ident % 2 == 0, both[:8], both[8:])

    for pair in range(pairs):
        peer = (base + pair) * 2
        rows = jnp.concatenate([block(peer), block(peer + 1)], axis=0)
        out_ref[pair * 16 : pair * 16 + 16, :] = rows.astype(BF16)


def local_kernel(widths, starts, block_count, p_ref, q_ref, pos_ref, neg_ref, tot_ref, spos_ref, bias_ref):
    rows = p_ref.shape[0]
    cols = q_ref.shape[0]
    chunk = min(256, rows)
    pos = pos_ref[0:1, :]
    for k in range(3):
        span = slice(starts[k], starts[k] + widths[k])
        q = q_ref[:, span]
        tot = jnp.zeros((1, cols), F32)
        spos = jnp.zeros((1, cols), F32)
        for at in range(0, rows, chunk):
            s = lax.dot_general(p_ref[at : at + chunk, span], q, NT, preferred_element_type=F32)
            row = lax.broadcasted_iota(jnp.int32, (chunk, cols), 0) + at
            tot = tot + jnp.sum(jnp.exp2(s * EXP_SCALE), axis=0, keepdims=True)
            spos = spos + jnp.sum(jnp.where(row == pos, s, 0.0), axis=0, keepdims=True)
        tot_ref[k : k + 1, :] = tot
        spos_ref[k : k + 1, :] = spos * SHARPNESS
    @pl.when(pl.program_id(0) == 0)
    def _():
        far = bias_ref.shape[0]
        lists, entries = neg_ref.shape
        peer = lax.broadcasted_iota(jnp.int32, (far, entries), 0) // PROWS
        lane = lax.broadcasted_iota(jnp.int32, bias_ref.shape, 1)
        bias = jnp.full(bias_ref.shape, OFF, F32)
        for b in range(lists):
            local_ids = jnp.broadcast_to(neg_ref[b : b + 1, :], (far, entries)) - peer * block_count
            hit = (local_ids >= 0) & (local_ids < block_count)
            listed = jnp.max(jnp.where(hit, 1.0, 0.0), axis=1, keepdims=True)
            bias = jnp.where((lane == b) & (listed > 0.0), 0.0, bias)
        bias_ref[...] = bias


def far_kernel(
    widths, starts, lists, far_any, q_any, bias_ref, tot_ref, spos_ref,
    term_any, g_any, scale_ref, loss_ref,
    far_v, q_v, e_v, g_v, term_v, in_sems, g_sems, term_sems,
):
    far, rows = g_v.shape[1], g_v.shape[2]
    cols = rows // lists
    chunk = min(256, far)
    order = (0, 1, 2)
    loads = {}
    for k in order:
        span = pl.ds(starts[k], widths[k])
        loads[k] = (
            pltpu.make_async_copy(far_any.at[:, span], far_v.at[:, span], in_sems.at[k, 0]),
            pltpu.make_async_copy(q_any.at[:, span], q_v.at[:, span], in_sems.at[k, 1]),
        )
        for load in loads[k]:
            load.start()
    stores = []
    loss = jnp.zeros((1, rows), F32)
    for k in order:
        span = slice(starts[k], starts[k] + widths[k])
        for load in loads[k]:
            load.wait()
        for b in range(lists):
            at_q = slice(b * cols, (b + 1) * cols)
            q = q_v[at_q, span]
            tot = tot_ref[k : k + 1, at_q]
            for at in range(0, far, chunk):
                s = lax.dot_general(far_v[at : at + chunk, span], q, NT, preferred_element_type=F32)
                bias = bias_ref[at : at + chunk, b : b + 1]
                e = jnp.exp2(s * EXP_SCALE + bias)
                tot = tot + jnp.sum(e, axis=0, keepdims=True)
                e_v[at : at + chunk, at_q] = e
            scale = SHARPNESS / tot
            scale_ref[k : k + 1, at_q] = scale
            loss_ref[k : k + 1, at_q] = jnp.log(tot) - spos_ref[k : k + 1, at_q]
            for at in range(0, far, chunk):
                g_v[k, at : at + chunk, at_q] = (e_v[at : at + chunk, at_q] * scale).astype(BF16)
        store = pltpu.make_async_copy(g_v.at[k], g_any.at[k], g_sems.at[k])
        store.start()
        stores.append(store)
        step = 256
        for at in range(0, widths[k], step):
            here = slice(starts[k] + at, starts[k] + at + step)
            for row in range(0, far, chunk):
                part = jnp.dot(g_v[k, row : row + chunk, :], q_v[:, here], preferred_element_type=F32)
                term_v[row : row + chunk, here] = part.astype(BF16)
        store = pltpu.make_async_copy(
            term_v.at[:, pl.ds(starts[k], widths[k])],
            term_any.at[:, pl.ds(starts[k], widths[k])],
            term_sems.at[k],
        )
        store.start()
        stores.append(store)
    for store in stores:
        store.wait()


def near_kernel(
    k, p_ref, q_ref, far_ref, g_ref, raw_ref, inv_ref, scale_ref, pos_ref, out_ref, dp_ref
):
    rows = p_ref.shape[0]
    cols = q_ref.shape[0]
    q = q_ref[...]
    pos = pos_ref[0:1, :]
    scale = scale_ref[k : k + 1, :]
    chunk = min(256, rows)
    first = pl.program_id(0) == 0
    dq = lax.dot_general(g_ref[0], far_ref[...], TN, preferred_element_type=F32)
    parts = []
    for at in range(0, rows, chunk):
        s = lax.dot_general(p_ref[at : at + chunk, :], q, NT, preferred_element_type=F32)
        row = lax.broadcasted_iota(jnp.int32, (chunk, cols), 0) + at
        g = jnp.exp2(s * EXP_SCALE) * scale
        parts.append((g - jnp.where(row == pos, SHARPNESS, 0.0)).astype(BF16))
    weights = jnp.concatenate(parts, axis=0)
    dq = dq + lax.dot_general(weights, p_ref[...], TN, preferred_element_type=F32)
    dp = jnp.dot(weights, q, preferred_element_type=F32)

    @pl.when(first)
    def _():
        dp_ref[...] = dp

    @pl.when(jnp.logical_not(first))
    def _():
        dp_ref[...] += dp

    inverse = inv_ref[:, k : k + 1]
    unit = raw_ref[...].astype(F32) * inverse
    out_ref[...] = (dq - unit * jnp.sum(unit * dq, axis=1, keepdims=True)) * inverse


def passage_kernel(
    widths, starts, place_ref, term_any, dp0, dp1, dp2, raw0, raw1, raw2, inv_ref,
    out0, out1, out2,
    term_v, pick_v, acc0, acc1, acc2, rv0, rv1, rv2, in_sems, out_sems,
):
    dps, raws, outs = (dp0, dp1, dp2), (raw0, raw1, raw2), (out0, out1, out2)
    accs, raw_vs = (acc0, acc1, acc2), (rv0, rv1, rv2)
    rows = acc0.shape[0]
    far = term_v.shape[0]
    order = (0, 1, 2)
    chunk = min(256, rows)
    loads = {}
    for k in order:
        span = pl.ds(starts[k], widths[k])
        loads[k] = (
            pltpu.make_async_copy(term_any.at[:, span], term_v.at[:, span], in_sems.at[k, 0]),
            pltpu.make_async_copy(dps[k], accs[k], in_sems.at[k, 1]),
            pltpu.make_async_copy(raws[k], raw_vs[k], in_sems.at[k, 2]),
        )
        for load in loads[k]:
            load.start()
    place = place_ref[0:1, :]
    for at in range(0, rows, chunk):
        row = lax.broadcasted_iota(jnp.int32, (chunk, far), 0) + at
        pick_v[at : at + chunk, :] = jnp.where(row == place, 1.0, 0.0).astype(BF16)
    stores = []
    for k in order:
        for load in loads[k]:
            load.wait()
        terms = term_v[:, starts[k] : starts[k] + widths[k]]
        for at in range(0, rows, chunk):
            here = slice(at, at + chunk)
            inverse = inv_ref[here, 3 + k : 4 + k]
            unit = raw_vs[k][here, :].astype(F32) * inverse
            dp = accs[k][here, :] + jnp.dot(pick_v[here, :], terms, preferred_element_type=F32)
            dot = jnp.sum(unit * dp, axis=1, keepdims=True)
            accs[k][here, :] = (dp - unit * dot) * inverse
            part = pl.ds(at, chunk)
            store = pltpu.make_async_copy(
                accs[k].at[part, :], outs[k].at[part, :], out_sems.at[k, at // chunk]
            )
            store.start()
            stores.append(store)
    for store in stores:
        store.wait()


def local(
    query_first, query_second, query_third,
    passage_first, passage_second, passage_third,
    neg_blocks, positives,
):
    devices = lax.axis_size(AXES)
    own = lax.axis_index(AXES)
    queries = (query_first, query_second, query_third)
    passages = (passage_first, passage_second, passage_third)
    widths = [values.shape[1] for values in queries]
    starts = columns_of(widths)
    wide = sum(widths)
    rows = query_first.shape[0]
    block_count = rows // PROWS
    lists, entries = neg_blocks.shape
    far = devices * PROWS
    cols = rows // lists
    params = functools.partial(pltpu.CompilerParams)

    wanted = pl.pallas_call(
        functools.partial(wanted_kernel, block_count),
        out_shape=jax.ShapeDtypeStruct((devices, LANES), jnp.int32),
        in_specs=[VMEM],
        out_specs=VMEM,
        compiler_params=params(vmem_limit_bytes=62 * MIB),
    )(neg_blocks)
    asked = exchange(wanted[:, None, :]).reshape(devices, LANES)

    step = rows // 8
    row_block = lambda width: pl.BlockSpec((step, width), lambda i: (i, 0))
    q_all, p_all, inverses = pl.pallas_call(
        functools.partial(heads_kernel, widths, starts),
        grid=(8,),
        out_shape=(
            jax.ShapeDtypeStruct((rows, wide), BF16),
            jax.ShapeDtypeStruct((rows, wide), BF16),
            jax.ShapeDtypeStruct((rows, LANES), F32),
        ),
        in_specs=[row_block(width) for width in widths + widths],
        out_specs=(row_block(wide), row_block(wide), row_block(LANES)),
        compiler_params=params(vmem_limit_bytes=62 * MIB),
        cost_estimate=cost(rows * wide * 8, rows * wide * 8),
    )(*queries, *passages)

    pairs = max(1, devices // 2 // 8)
    send = pl.pallas_call(
        functools.partial(gather_kernel, pairs),
        grid=(devices // 2 // pairs,),
        out_shape=jax.ShapeDtypeStruct((far, wide), BF16),
        in_specs=[SMEM, pl.BlockSpec((rows, wide), lambda i: (0, 0))],
        out_specs=pl.BlockSpec((pairs * 16, wide), lambda i: (i, 0)),
        compiler_params=params(vmem_limit_bytes=62 * MIB),
        cost_estimate=cost(far * wide, far * wide * 4),
    )(asked, p_all)
    fetched = exchange(send.reshape(devices, PROWS, wide)).reshape(far, wide)

    local_pos = (positives - own * rows).reshape(1, rows)
    whole = lambda shape: pl.BlockSpec(shape, lambda i: (0,) * len(shape))
    lane_block = pl.BlockSpec((8, cols), lambda i: (0, i))
    pos_block = pl.BlockSpec((1, cols), lambda i: (0, i))
    totals, positive_scores, bias = pl.pallas_call(
        functools.partial(local_kernel, widths, starts, block_count),
        grid=(lists,),
        out_shape=(
            jax.ShapeDtypeStruct((8, rows), F32),
            jax.ShapeDtypeStruct((8, rows), F32),
            jax.ShapeDtypeStruct((far, LANES), F32),
        ),
        in_specs=[
            whole((rows, wide)),
            pl.BlockSpec((cols, wide), lambda i: (i, 0)),
            pos_block,
            whole((lists, entries)),
        ],
        out_specs=(lane_block, lane_block, whole((far, LANES))),
        compiler_params=params(vmem_limit_bytes=62 * MIB),
        cost_estimate=cost(2 * rows * rows * wide, rows * wide * 4),
    )(p_all, q_all, local_pos, neg_blocks)

    terms, far_weights, scales, loss_rows = pl.pallas_call(
        functools.partial(far_kernel, widths, starts, lists),
        out_shape=(
            jax.ShapeDtypeStruct((far, wide), BF16),
            jax.ShapeDtypeStruct((3, far, rows), BF16),
            jax.ShapeDtypeStruct((8, rows), F32),
            jax.ShapeDtypeStruct((8, rows), F32),
        ),
        in_specs=[HBM, HBM, VMEM, VMEM, VMEM],
        out_specs=(HBM, HBM, VMEM, VMEM),
        scratch_shapes=[
            pltpu.VMEM((far, wide), BF16),
            pltpu.VMEM((rows, wide), BF16),
            pltpu.VMEM((far, rows), F32),
            pltpu.VMEM((3, far, rows), BF16),
            pltpu.VMEM((far, wide), BF16),
            pltpu.SemaphoreType.DMA((3, 2)),
            pltpu.SemaphoreType.DMA((3,)),
            pltpu.SemaphoreType.DMA((3,)),
        ],
        compiler_params=params(vmem_limit_bytes=62 * MIB),
        cost_estimate=cost(4 * far * rows * wide, 6 * far * wide),
    )(fetched, q_all, bias, totals, positive_scores)
    losses = loss_rows[0] + loss_rows[1] + loss_rows[2]
    returned = exchange(terms.reshape(devices, PROWS, wide)).reshape(far, wide)

    q_grads = []
    dp_parts = []
    for k in range(3):
        width = widths[k]
        place = starts[k] // width
        q_grad, dp_part = pl.pallas_call(
            functools.partial(near_kernel, k),
            grid=(lists,),
            out_shape=(
                jax.ShapeDtypeStruct((rows, width), F32),
                jax.ShapeDtypeStruct((rows, width), F32),
            ),
            in_specs=[
                pl.BlockSpec((rows, width), lambda i, place=place: (0, place)),
                pl.BlockSpec((cols, width), lambda i, place=place: (i, place)),
                pl.BlockSpec((far, width), lambda i, place=place: (0, place)),
                pl.BlockSpec((1, far, cols), lambda i, k=k: (k, 0, i)),
                pl.BlockSpec((cols, width), lambda i: (i, 0)),
                pl.BlockSpec((cols, LANES), lambda i: (i, 0)),
                lane_block,
                pos_block,
            ],
            out_specs=(
                pl.BlockSpec((cols, width), lambda i: (i, 0)),
                pl.BlockSpec((rows, width), lambda i: (0, 0)),
            ),
            compiler_params=params(vmem_limit_bytes=62 * MIB),
            cost_estimate=cost(8 * rows * rows * width, 16 * rows * width),
        )(p_all, q_all, fetched, far_weights, queries[k], inverses, scales, local_pos)
        q_grads.append(q_grad)
        dp_parts.append(dp_part)

    offsets = jnp.arange(PROWS, dtype=jnp.int32)
    asked_ids = asked[:, :1]
    place = jnp.where(asked_ids >= 0, asked_ids * PROWS + offsets[None, :], -1).reshape(1, far)
    p_grads = pl.pallas_call(
        functools.partial(passage_kernel, widths, starts),
        out_shape=tuple(jax.ShapeDtypeStruct((rows, width), F32) for width in widths),
        in_specs=[VMEM] + [HBM] * 7 + [VMEM],
        out_specs=(HBM, HBM, HBM),
        scratch_shapes=[pltpu.VMEM((far, wide), BF16), pltpu.VMEM((rows, far), BF16)]
        + [pltpu.VMEM((rows, width), F32) for width in widths]
        + [pltpu.VMEM((rows, width), BF16) for width in widths]
        + [pltpu.SemaphoreType.DMA((3, 3)), pltpu.SemaphoreType.DMA((3, 4))],
        compiler_params=params(vmem_limit_bytes=62 * MIB),
        cost_estimate=cost(16 * rows * wide, 12 * rows * wide),
    )(place, returned, *dp_parts, *passages, inverses)
    return (losses, *q_grads, *p_grads)


def solution(mesh):
    rows = P(AXES, None)
    return jax.shard_map(
        local,
        mesh=mesh,
        in_specs=(rows,) * 7 + (P(AXES),),
        out_specs=(P(AXES),) + (rows,) * 6,
        check_vma=False,
    )
```

```python
import functools
import math

import jax
import jax.numpy as jnp
from jax import lax
from jax.experimental import pallas as pl
from jax.experimental.pallas import tpu as pltpu
from jax.sharding import PartitionSpec as P

PROWS = 8
LANES = 128
AXES = ("dp", "group")

EPSILON = 1e-06
SHARPNESS = 20.0
EXP_SCALE = SHARPNESS * math.log2(math.e)
OFF = -1e30

F32 = jnp.float32
BF16 = jnp.bfloat16
HBM = pl.BlockSpec(memory_space=pltpu.HBM)
VMEM = pl.BlockSpec(memory_space=pltpu.VMEM)
SMEM = pl.BlockSpec(memory_space=pltpu.SMEM)
MIB = 1024 * 1024
NT = (((1,), (1,)), ((), ()))
TN = (((0,), (0,)), ((), ()))
NN = (((1,), (0,)), ((), ()))


def exchange(values):
    return lax.all_to_all(values, AXES, split_axis=0, concat_axis=0, tiled=True)


def cost(flops, moved):
    return pl.CostEstimate(flops=int(flops), bytes_accessed=int(moved), transcendentals=0)


def columns_of(widths):
    starts = {}
    at = 0
    for index in sorted(range(len(widths)), key=lambda i: -widths[i]):
        starts[index] = at
        at += widths[index]
    return [starts[i] for i in range(len(widths))]


def wanted_kernel(block_count, neg_ref, out_ref):
    peers = out_ref.shape[0]
    lists, entries = neg_ref.shape
    peer = lax.broadcasted_iota(jnp.int32, (peers, entries), 0)
    best = jnp.full((peers, 1), -1, jnp.int32)
    for row in range(lists):
        ids = jnp.broadcast_to(neg_ref[row : row + 1, :], (peers, entries))
        local_ids = ids - peer * block_count
        hit = (local_ids >= 0) & (local_ids < block_count)
        best = jnp.maximum(best, jnp.max(jnp.where(hit, local_ids, -1), axis=1, keepdims=True))
    out_ref[...] = jnp.broadcast_to(best, out_ref.shape)


def heads_kernel(widths, starts, raw0, raw1, raw2, after_ref, out_ref, inv_ref):
    del after_ref
    lane = lax.broadcasted_iota(jnp.int32, inv_ref.shape, 1)
    packed = jnp.zeros(inv_ref.shape, F32)
    for k, raw in enumerate((raw0, raw1, raw2)):
        values = raw[...].astype(F32)
        inverse = lax.rsqrt(jnp.sum(values * values, axis=1, keepdims=True) + EPSILON)
        out_ref[:, starts[k] : starts[k] + widths[k]] = (values * inverse).astype(BF16)
        packed = jnp.where(lane == k, inverse, packed)
    inv_ref[...] = packed


def gather_kernel(asked_ref, p_ref, out_hbm, out_v, sems):
    pairs = out_v.shape[0] // 16
    parts = min(8, pairs)
    each = pairs // parts

    def block(peer):
        ident = jnp.maximum(asked_ref[peer, 0], 0)
        start = pl.multiple_of((ident // 2) * 16, 16)
        both = p_ref[pl.ds(start, 16), :].astype(F32)
        return jnp.where(ident % 2 == 0, both[:8], both[8:])

    stores = []
    for part in range(parts):
        for pair in range(part * each, (part + 1) * each):
            rows = jnp.concatenate([block(pair * 2), block(pair * 2 + 1)], axis=0)
            out_v[pair * 16 : pair * 16 + 16, :] = rows.astype(BF16)
        here = pl.ds(part * each * 16, each * 16)
        store = pltpu.make_async_copy(out_v.at[here, :], out_hbm.at[here, :], sems.at[part])
        store.start()
        stores.append(store)
    for store in stores:
        store.wait()


def local_kernel(
    widths, starts, block_count, p_ref, q_ref, pos_ref, neg_ref,
    tot_ref, spos_ref, bias_ref, e_ref,
):
    rows = p_ref.shape[0]
    cols = pos_ref.shape[1]
    chunk = min(256, rows)
    pos = pos_ref[0:1, :]
    for k in range(3):
        span = slice(starts[k], starts[k] + widths[k])
        q = q_ref[:, span]
        tot = jnp.zeros((1, cols), F32)
        spos = jnp.zeros((1, cols), F32)
        for at in range(0, rows, chunk):
            s = lax.dot_general(p_ref[at : at + chunk, span], q, NT, preferred_element_type=F32)
            row = lax.broadcasted_iota(jnp.int32, (chunk, cols), 0) + at
            e = jnp.exp2(s * EXP_SCALE)
            e_ref[k, at : at + chunk, :] = e.astype(BF16)
            tot = tot + jnp.sum(e, axis=0, keepdims=True)
            spos = spos + jnp.sum(jnp.where(row == pos, s, 0.0), axis=0, keepdims=True)
        tot_ref[k : k + 1, :] = tot
        spos_ref[k : k + 1, :] = spos * SHARPNESS
    @pl.when(pl.program_id(0) == 0)
    def _():
        far = bias_ref.shape[0]
        lists, entries = neg_ref.shape
        peer = lax.broadcasted_iota(jnp.int32, (far, entries), 0) // PROWS
        lane = lax.broadcasted_iota(jnp.int32, bias_ref.shape, 1)
        bias = jnp.full(bias_ref.shape, OFF, F32)
        for b in range(lists):
            local_ids = jnp.broadcast_to(neg_ref[b : b + 1, :], (far, entries)) - peer * block_count
            hit = (local_ids >= 0) & (local_ids < block_count)
            listed = jnp.max(jnp.where(hit, 1.0, 0.0), axis=1, keepdims=True)
            bias = jnp.where((lane == b) & (listed > 0.0), 0.0, bias)
        bias_ref[...] = bias


def far_kernel(
    widths, starts, lists, far_hbm, q_hbm, bias_ref, tot_ref, spos_ref,
    term_hbm, scale_ref, loss_ref,
    far_ref, q_ref, g_ref, e_v, term_v, in_sems, out_sems,
):
    far, rows = g_ref.shape
    cols = rows // lists
    chunk = min(256, far)
    order = (0, 1, 2)
    loads = {}
    for k in order:
        span = pl.ds(starts[k], widths[k])
        loads[k] = (
            pltpu.make_async_copy(far_hbm.at[:, span], far_ref.at[:, span], in_sems.at[k, 0]),
            pltpu.make_async_copy(q_hbm.at[:, span], q_ref.at[:, span], in_sems.at[k, 1]),
        )
        for load in loads[k]:
            load.start()
    stores = []
    step = 256
    for k in order:
        span = slice(starts[k], starts[k] + widths[k])
        for load in loads[k]:
            load.wait()
        for b in range(lists):
            at_q = slice(b * cols, (b + 1) * cols)
            q = q_ref[at_q, span]
            tot = tot_ref[k : k + 1, at_q]
            for at in range(0, far, chunk):
                s = lax.dot_general(far_ref[at : at + chunk, span], q, NT, preferred_element_type=F32)
                bias = bias_ref[at : at + chunk, b : b + 1]
                e = jnp.exp2(s * EXP_SCALE + bias)
                tot = tot + jnp.sum(e, axis=0, keepdims=True)
                e_v[at : at + chunk, at_q] = e
            scale = SHARPNESS / tot
            scale_ref[k : k + 1, at_q] = scale
            loss_ref[k : k + 1, at_q] = jnp.log(tot) - spos_ref[k : k + 1, at_q]
            for at in range(0, far, chunk):
                g_ref[at : at + chunk, at_q] = (e_v[at : at + chunk, at_q] * scale).astype(BF16)
        for at in range(starts[k], starts[k] + widths[k], step):
            here = slice(at, at + step)
            for row in range(0, far, chunk):
                part = jnp.dot(g_ref[row : row + chunk, :], q_ref[:, here], preferred_element_type=F32)
                term_v[row : row + chunk, here] = part.astype(BF16)
            here = pl.ds(at, step)
            store = pltpu.make_async_copy(
                term_v.at[:, here], term_hbm.at[:, here], out_sems.at[at // step]
            )
            store.start()
            stores.append(store)
    for store in stores:
        store.wait()


def raw_gradient(raw, inverse, grad):
    unit = raw.astype(F32) * inverse
    return (grad - unit * jnp.sum(unit * grad, axis=1, keepdims=True)) * inverse


def near_kernel(
    k, lists, p_ref, q_ref, far_ref, e_ref, raw_ref, inv_ref, scale_ref, bias_ref, pos_ref,
    p_raw_ref, p_inv_ref, out_ref, part_ref, dp_v,
):
    rows = p_ref.shape[0]
    far = far_ref.shape[0]
    cols = q_ref.shape[0]
    q = q_ref[...]
    pos = pos_ref[0:1, :]
    scale = scale_ref[k : k + 1, :]
    chunk = min(256, rows, far)
    step = pl.program_id(0)
    lane = lax.broadcasted_iota(jnp.int32, (chunk, LANES), 1)
    parts = []
    for at in range(0, far, chunk):
        s = lax.dot_general(far_ref[at : at + chunk, :], q, NT, preferred_element_type=F32)
        bias = jnp.sum(jnp.where(lane == step, bias_ref[at : at + chunk, :], 0.0), axis=1, keepdims=True)
        parts.append((jnp.exp2(s * EXP_SCALE + bias) * scale).astype(BF16))
    dq = lax.dot_general(
        jnp.concatenate(parts, axis=0), far_ref[...], TN, preferred_element_type=F32
    )
    parts = []
    for at in range(0, rows, chunk):
        row = lax.broadcasted_iota(jnp.int32, (chunk, cols), 0) + at
        g = e_ref[0, at : at + chunk, :].astype(F32) * scale
        parts.append((g - jnp.where(row == pos, SHARPNESS, 0.0)).astype(BF16))
    weights = jnp.concatenate(parts, axis=0)
    dq = dq + lax.dot_general(weights, p_ref[...], TN, preferred_element_type=F32)
    dp = jnp.dot(weights, q, preferred_element_type=F32)

    @pl.when(step == 0)
    def _():
        dp_v[...] = dp

    @pl.when(step > 0)
    def _():
        dp_v[...] += dp

    out_ref[...] = raw_gradient(raw_ref[...], inv_ref[:, k : k + 1], dq)

    @pl.when(step == lists - 1)
    def _():
        for at in range(0, rows, chunk):
            here = slice(at, at + chunk)
            part = raw_gradient(p_raw_ref[here, :], p_inv_ref[here, k : k + 1], dp_v[here, :])
            part_ref[here, :] = part.astype(BF16)


def passage_kernel(
    widths, starts, place_ref, term_hbm, part0, part1, part2, raw0, raw1, raw2, inv_ref,
    out0, out1, out2,
    term_v, pick_v, dv0, dv1, dv2, rv0, rv1, rv2, ov0, ov1, ov2, in_sems, out_sems,
):
    parts, raws, outs = (part0, part1, part2), (raw0, raw1, raw2), (out0, out1, out2)
    part_vs, raw_vs, out_vs = (dv0, dv1, dv2), (rv0, rv1, rv2), (ov0, ov1, ov2)
    rows = ov0.shape[0]
    far = term_v.shape[0]
    order = (0, 1, 2)
    chunk = min(256, rows)
    loads = {}
    for k in order:
        span = pl.ds(starts[k], widths[k])
        loads[k] = (
            pltpu.make_async_copy(term_hbm.at[:, span], term_v.at[:, span], in_sems.at[k, 0]),
            pltpu.make_async_copy(parts[k], part_vs[k], in_sems.at[k, 1]),
            pltpu.make_async_copy(raws[k], raw_vs[k], in_sems.at[k, 2]),
        )
        for load in loads[k]:
            load.start()
    place = place_ref[0:1, :]
    for at in range(0, rows, chunk):
        row = lax.broadcasted_iota(jnp.int32, (chunk, far), 0) + at
        pick_v[at : at + chunk, :] = jnp.where(row == place, 1.0, 0.0).astype(BF16)
    stores = []
    for k in order:
        for load in loads[k]:
            load.wait()
        terms = term_v[:, starts[k] : starts[k] + widths[k]]
        for at in range(0, rows, chunk):
            here = slice(at, at + chunk)
            inverse = inv_ref[here, k : k + 1]
            added = jnp.dot(pick_v[here, :], terms, preferred_element_type=F32)
            added = raw_gradient(raw_vs[k][here, :], inverse, added)
            out_vs[k][here, :] = part_vs[k][here, :].astype(F32) + added
            part = pl.ds(at, chunk)
            store = pltpu.make_async_copy(
                out_vs[k].at[part, :], outs[k].at[part, :], out_sems.at[k, at // chunk]
            )
            store.start()
            stores.append(store)
    for store in stores:
        store.wait()


def local(
    query_first, query_second, query_third,
    passage_first, passage_second, passage_third,
    neg_blocks, positives,
):
    devices = lax.axis_size(AXES)
    own = lax.axis_index(AXES)
    queries = (query_first, query_second, query_third)
    passages = (passage_first, passage_second, passage_third)
    widths = [values.shape[1] for values in queries]
    starts = columns_of(widths)
    wide = sum(widths)
    rows = query_first.shape[0]
    block_count = rows // PROWS
    lists, entries = neg_blocks.shape
    far = devices * PROWS
    cols = rows // lists
    params = pltpu.CompilerParams(vmem_limit_bytes=62 * MIB)
    shape = jax.ShapeDtypeStruct

    wanted = pl.pallas_call(
        functools.partial(wanted_kernel, block_count),
        out_shape=jax.ShapeDtypeStruct((devices, LANES), jnp.int32),
        in_specs=[VMEM],
        out_specs=VMEM,
        compiler_params=params,
    )(neg_blocks)
    asked = exchange(wanted[:, None, :]).reshape(devices, LANES)

    step = rows // 4
    row_block = lambda width: pl.BlockSpec((step, width), lambda i: (i, 0))

    def heads(values, after):
        return pl.pallas_call(
            functools.partial(heads_kernel, widths, starts),
            grid=(4,),
            out_shape=(shape((rows, wide), BF16), shape((rows, LANES), F32)),
            in_specs=[row_block(width) for width in widths] + [HBM],
            out_specs=(row_block(wide), row_block(LANES)),
            compiler_params=params,
            cost_estimate=cost(rows * wide * 4, rows * wide * 4),
        )(*values, after)

    p_all, p_inverses = heads(passages, wanted)

    send = pl.pallas_call(
        gather_kernel,
        out_shape=shape((far, wide), BF16),
        in_specs=[SMEM, VMEM],
        out_specs=HBM,
        scratch_shapes=[pltpu.VMEM((far, wide), BF16), pltpu.SemaphoreType.DMA((8,))],
        compiler_params=params,
        cost_estimate=cost(far * wide, far * wide * 4),
    )(asked, p_all)
    fetched = exchange(send.reshape(devices, PROWS, wide)).reshape(far, wide)

    q_all, q_inverses = heads(queries, send)
    local_pos = (positives - own * rows).reshape(1, rows)
    whole = lambda dims: pl.BlockSpec(dims, lambda i: (0,) * len(dims))
    pos_block = pl.BlockSpec((1, cols), lambda i: (0, i))
    lane_block = pl.BlockSpec((8, cols), lambda i: (0, i))
    totals, positive_scores, bias, local_exps = pl.pallas_call(
        functools.partial(local_kernel, widths, starts, block_count),
        grid=(lists,),
        out_shape=(
            shape((8, rows), F32),
            shape((8, rows), F32),
            shape((far, LANES), F32),
            shape((3, rows, rows), BF16),
        ),
        in_specs=[
            whole((rows, wide)),
            pl.BlockSpec((cols, wide), lambda i: (i, 0)),
            pos_block,
            whole((lists, entries)),
        ],
        out_specs=(
            lane_block,
            lane_block,
            whole((far, LANES)),
            pl.BlockSpec((3, rows, cols), lambda i: (0, 0, i)),
        ),
        compiler_params=params,
        cost_estimate=cost(2 * rows * rows * wide, rows * wide * 4),
    )(p_all, q_all, local_pos, neg_blocks)

    terms, scales, loss_rows = pl.pallas_call(
        functools.partial(far_kernel, widths, starts, lists),
        out_shape=(shape((far, wide), BF16), shape((8, rows), F32), shape((8, rows), F32)),
        in_specs=[HBM, HBM, VMEM, VMEM, VMEM],
        out_specs=(HBM, VMEM, VMEM),
        scratch_shapes=[
            pltpu.VMEM((far, wide), BF16),
            pltpu.VMEM((rows, wide), BF16),
            pltpu.VMEM((far, rows), BF16),
            pltpu.VMEM((far, rows), F32),
            pltpu.VMEM((far, wide), BF16),
            pltpu.SemaphoreType.DMA((3, 2)),
            pltpu.SemaphoreType.DMA((wide // 256,)),
        ],
        compiler_params=params,
        cost_estimate=cost(4 * far * rows * wide, 6 * far * wide),
    )(fetched, q_all, bias, totals, positive_scores)
    losses = loss_rows[0] + loss_rows[1] + loss_rows[2]
    returned = exchange(terms.reshape(devices, PROWS, wide)).reshape(far, wide)

    q_grads = []
    p_parts = []
    for k in range(3):
        width = widths[k]
        place = starts[k] // width
        q_grad, p_part = pl.pallas_call(
            functools.partial(near_kernel, k, lists),
            grid=(lists,),
            out_shape=(shape((rows, width), F32), shape((rows, width), BF16)),
            in_specs=[
                pl.BlockSpec((rows, width), lambda i, place=place: (0, place)),
                pl.BlockSpec((cols, width), lambda i, place=place: (i, place)),
                pl.BlockSpec((far, width), lambda i, place=place: (0, place)),
                pl.BlockSpec((1, rows, cols), lambda i, k=k: (k, 0, i)),
                pl.BlockSpec((cols, width), lambda i: (i, 0)),
                pl.BlockSpec((cols, LANES), lambda i: (i, 0)),
                lane_block,
                whole((far, LANES)),
                pos_block,
                whole((rows, width)),
                whole((rows, LANES)),
            ],
            out_specs=(pl.BlockSpec((cols, width), lambda i: (i, 0)), whole((rows, width))),
            scratch_shapes=[pltpu.VMEM((rows, width), F32)],
            compiler_params=params,
            cost_estimate=cost(8 * rows * rows * width, 16 * rows * width),
        )(
            p_all, q_all, fetched, local_exps, queries[k], q_inverses, scales, bias, local_pos,
            passages[k], p_inverses,
        )
        q_grads.append(q_grad)
        p_parts.append(p_part)

    offsets = jnp.arange(PROWS, dtype=jnp.int32)
    asked_ids = asked[:, :1]
    place = jnp.where(asked_ids >= 0, asked_ids * PROWS + offsets[None, :], -1).reshape(1, far)
    p_grads = pl.pallas_call(
        functools.partial(passage_kernel, widths, starts),
        out_shape=tuple(shape((rows, width), F32) for width in widths),
        in_specs=[VMEM] + [HBM] * 7 + [VMEM],
        out_specs=(HBM, HBM, HBM),
        scratch_shapes=[pltpu.VMEM((far, wide), BF16), pltpu.VMEM((rows, far), BF16)]
        + [pltpu.VMEM((rows, width), BF16) for width in widths]
        + [pltpu.VMEM((rows, width), BF16) for width in widths]
        + [pltpu.VMEM((rows, width), F32) for width in widths]
        + [pltpu.SemaphoreType.DMA((3, 3)), pltpu.SemaphoreType.DMA((3, 4))],
        compiler_params=params,
        cost_estimate=cost(16 * rows * wide, 12 * rows * wide),
    )(place, returned, *p_parts, *passages, p_inverses)
    return (losses, *q_grads, *p_grads)


def solution(mesh):
    rows = P(AXES, None)
    return jax.shard_map(
        local,
        mesh=mesh,
        in_specs=(rows,) * 7 + (P(AXES),),
        out_specs=(P(AXES),) + (rows,) * 6,
        check_vma=False,
    )
```

```python
import functools
import math

import jax
import jax.numpy as jnp
from jax import lax
from jax.experimental import pallas as pl
from jax.experimental.pallas import tpu as pltpu
from jax.sharding import PartitionSpec as P

PROWS = 8
LANES = 128
AXES = ("dp", "group")

EPSILON = 1e-06
SHARPNESS = 20.0
EXP_SCALE = SHARPNESS * math.log2(math.e)
OFF = -1e30

F32 = jnp.float32
BF16 = jnp.bfloat16
HBM = pl.BlockSpec(memory_space=pltpu.HBM)
VMEM = pl.BlockSpec(memory_space=pltpu.VMEM)
SMEM = pl.BlockSpec(memory_space=pltpu.SMEM)
MIB = 1024 * 1024
NT = (((1,), (1,)), ((), ()))
TN = (((0,), (0,)), ((), ()))
NN = (((1,), (0,)), ((), ()))


def exchange(values):
    return lax.all_to_all(values, AXES, split_axis=0, concat_axis=0, tiled=True)


def cost(flops, moved):
    return pl.CostEstimate(flops=int(flops), bytes_accessed=int(moved), transcendentals=0)


def columns_of(widths):
    starts = {}
    at = 0
    for index in sorted(range(len(widths)), key=lambda i: -widths[i]):
        starts[index] = at
        at += widths[index]
    return [starts[i] for i in range(len(widths))]


def wanted_kernel(block_count, neg_ref, out_ref):
    peers = out_ref.shape[0]
    lists, entries = neg_ref.shape
    peer = lax.broadcasted_iota(jnp.int32, (peers, entries), 0)
    best = jnp.full((peers, 1), -1, jnp.int32)
    for row in range(lists):
        ids = jnp.broadcast_to(neg_ref[row : row + 1, :], (peers, entries))
        local_ids = ids - peer * block_count
        hit = (local_ids >= 0) & (local_ids < block_count)
        best = jnp.maximum(best, jnp.max(jnp.where(hit, local_ids, -1), axis=1, keepdims=True))
    out_ref[...] = jnp.broadcast_to(best, out_ref.shape)


def heads_kernel(widths, starts, raw0, raw1, raw2, after_ref, out_ref, inv_ref):
    del after_ref
    lane = lax.broadcasted_iota(jnp.int32, inv_ref.shape, 1)
    packed = jnp.zeros(inv_ref.shape, F32)
    for k, raw in enumerate((raw0, raw1, raw2)):
        values = raw[...].astype(F32)
        inverse = lax.rsqrt(jnp.sum(values * values, axis=1, keepdims=True) + EPSILON)
        out_ref[:, starts[k] : starts[k] + widths[k]] = (values * inverse).astype(BF16)
        packed = jnp.where(lane == k, inverse, packed)
    inv_ref[...] = packed


def gather_kernel(asked_ref, p_ref, out_hbm, out_v, sems):
    pairs = out_v.shape[0] // 16
    parts = min(8, pairs)
    each = pairs // parts

    def block(peer):
        ident = jnp.maximum(asked_ref[peer, 0], 0)
        start = pl.multiple_of((ident // 2) * 16, 16)
        both = p_ref[pl.ds(start, 16), :].astype(F32)
        return jnp.where(ident % 2 == 0, both[:8], both[8:])

    stores = []
    for part in range(parts):
        for pair in range(part * each, (part + 1) * each):
            rows = jnp.concatenate([block(pair * 2), block(pair * 2 + 1)], axis=0)
            out_v[pair * 16 : pair * 16 + 16, :] = rows.astype(BF16)
        here = pl.ds(part * each * 16, each * 16)
        store = pltpu.make_async_copy(out_v.at[here, :], out_hbm.at[here, :], sems.at[part])
        store.start()
        stores.append(store)
    for store in stores:
        store.wait()


def local_kernel(
    widths, starts, block_count, p_ref, q_ref, pos_ref, neg_ref,
    tot_ref, spos_ref, bias_ref, e_ref,
):
    rows = p_ref.shape[0]
    cols = pos_ref.shape[1]
    chunk = min(256, rows)
    pos = pos_ref[0:1, :]
    for k in range(3):
        span = slice(starts[k], starts[k] + widths[k])
        q = q_ref[:, span]
        tot = jnp.zeros((1, cols), F32)
        spos = jnp.zeros((1, cols), F32)
        for at in range(0, rows, chunk):
            s = lax.dot_general(p_ref[at : at + chunk, span], q, NT, preferred_element_type=F32)
            row = lax.broadcasted_iota(jnp.int32, (chunk, cols), 0) + at
            e = jnp.exp2(s * EXP_SCALE)
            e_ref[k, at : at + chunk, :] = e.astype(BF16)
            tot = tot + jnp.sum(e, axis=0, keepdims=True)
            spos = spos + jnp.sum(jnp.where(row == pos, s, 0.0), axis=0, keepdims=True)
        tot_ref[k : k + 1, :] = tot
        spos_ref[k : k + 1, :] = spos * SHARPNESS
    @pl.when(pl.program_id(0) == 0)
    def _():
        far = bias_ref.shape[0]
        lists, entries = neg_ref.shape
        peer = lax.broadcasted_iota(jnp.int32, (far, entries), 0) // PROWS
        lane = lax.broadcasted_iota(jnp.int32, bias_ref.shape, 1)
        bias = jnp.full(bias_ref.shape, OFF, F32)
        for b in range(lists):
            local_ids = jnp.broadcast_to(neg_ref[b : b + 1, :], (far, entries)) - peer * block_count
            hit = (local_ids >= 0) & (local_ids < block_count)
            listed = jnp.max(jnp.where(hit, 1.0, 0.0), axis=1, keepdims=True)
            bias = jnp.where((lane == b) & (listed > 0.0), 0.0, bias)
        bias_ref[...] = bias


def far_scratch(far, rows, wide):
    return [
        pltpu.VMEM((far, wide), BF16),
        pltpu.VMEM((rows, wide), BF16),
        pltpu.VMEM((far, LANES), F32),
        pltpu.VMEM((8, rows), F32),
        pltpu.VMEM((8, rows), F32),
        pltpu.VMEM((8, rows), F32),
        pltpu.VMEM((8, rows), F32),
        pltpu.VMEM((far, rows), BF16),
        pltpu.VMEM((far, rows), F32),
        pltpu.VMEM((far, wide), BF16),
        pltpu.SemaphoreType.DMA((4, 3)),
        pltpu.SemaphoreType.DMA((4, 4)),
    ]


def far_kernel(
    widths, starts, lists, far_hbm, q_hbm, bias_hbm, tot_hbm, spos_hbm,
    term_hbm, scale_hbm, loss_hbm,
    far_ref, q_ref, bias_ref, tot_ref, spos_ref, scale_ref, loss_ref,
    g_ref, e_v, term_v, in_sems, out_sems,
):
    far, rows = g_ref.shape
    cols = rows // lists
    chunk = min(256, far)
    order = (0, 1, 2)
    loads = {}
    for k in order:
        span = pl.ds(starts[k], widths[k])
        loads[k] = [
            pltpu.make_async_copy(far_hbm.at[:, span], far_ref.at[:, span], in_sems.at[k, 0]),
            pltpu.make_async_copy(q_hbm.at[:, span], q_ref.at[:, span], in_sems.at[k, 1]),
        ]
        if k == order[0]:
            loads[k] += [
                pltpu.make_async_copy(bias_hbm, bias_ref, in_sems.at[3, 0]),
                pltpu.make_async_copy(tot_hbm, tot_ref, in_sems.at[3, 1]),
                pltpu.make_async_copy(spos_hbm, spos_ref, in_sems.at[3, 2]),
            ]
        for load in loads[k]:
            load.start()
    scale_ref[3:8, :] = jnp.zeros((5, rows), F32)
    loss_ref[3:8, :] = jnp.zeros((5, rows), F32)
    stores = []
    for k in order:
        span = slice(starts[k], starts[k] + widths[k])
        for load in loads[k]:
            load.wait()
        for b in range(lists):
            at_q = slice(b * cols, (b + 1) * cols)
            q = q_ref[at_q, span]
            tot = tot_ref[k : k + 1, at_q]
            for at in range(0, far, chunk):
                s = lax.dot_general(far_ref[at : at + chunk, span], q, NT, preferred_element_type=F32)
                bias = bias_ref[at : at + chunk, b : b + 1]
                e = jnp.exp2(s * EXP_SCALE + bias)
                tot = tot + jnp.sum(e, axis=0, keepdims=True)
                e_v[at : at + chunk, at_q] = e
            scale = SHARPNESS / tot
            scale_ref[k : k + 1, at_q] = scale
            loss_ref[k : k + 1, at_q] = jnp.log(tot) - spos_ref[k : k + 1, at_q]
            for at in range(0, far, chunk):
                g_ref[at : at + chunk, at_q] = (e_v[at : at + chunk, at_q] * scale).astype(BF16)
        if k == order[-1]:
            for index, (ref, hbm) in enumerate(((scale_ref, scale_hbm), (loss_ref, loss_hbm))):
                stores.append(pltpu.make_async_copy(ref, hbm, out_sems.at[3, index]))
                stores[-1].start()
        for row in range(0, far, chunk):
            here = slice(row, row + chunk)
            part = jnp.dot(g_ref[here, :], q_ref[:, span], preferred_element_type=F32)
            unit = far_ref[here, span].astype(F32)
            part = part - unit * jnp.sum(unit * part, axis=1, keepdims=True)
            term_v[here, span] = part.astype(BF16)
            place = (pl.ds(row, chunk), pl.ds(starts[k], widths[k]))
            store = pltpu.make_async_copy(
                term_v.at[place], term_hbm.at[place], out_sems.at[k, row // chunk]
            )
            store.start()
            stores.append(store)
    for store in stores:
        store.wait()


def raw_gradient(raw, inverse, grad):
    unit = raw.astype(F32) * inverse
    return (grad - unit * jnp.sum(unit * grad, axis=1, keepdims=True)) * inverse


def near_kernel(
    k, lists, p_ref, q_ref, far_ref, e_ref, raw_ref, inv_ref, scale_ref, bias_ref, pos_ref,
    p_raw_ref, p_inv_ref, out_ref, part_ref, dp_v,
):
    rows = p_ref.shape[0]
    far = far_ref.shape[0]
    cols = q_ref.shape[0]
    q = q_ref[...]
    pos = pos_ref[0:1, :]
    scale = scale_ref[k : k + 1, :]
    chunk = min(256, rows, far)
    step = pl.program_id(0)
    lane = lax.broadcasted_iota(jnp.int32, (chunk, LANES), 1)
    parts = []
    for at in range(0, far, chunk):
        s = lax.dot_general(far_ref[at : at + chunk, :], q, NT, preferred_element_type=F32)
        bias = jnp.sum(jnp.where(lane == step, bias_ref[at : at + chunk, :], 0.0), axis=1, keepdims=True)
        parts.append((jnp.exp2(s * EXP_SCALE + bias) * scale).astype(BF16))
    dq = lax.dot_general(
        jnp.concatenate(parts, axis=0), far_ref[...], TN, preferred_element_type=F32
    )
    parts = []
    for at in range(0, rows, chunk):
        row = lax.broadcasted_iota(jnp.int32, (chunk, cols), 0) + at
        g = e_ref[0, at : at + chunk, :].astype(F32) * scale
        parts.append((g - jnp.where(row == pos, SHARPNESS, 0.0)).astype(BF16))
    weights = jnp.concatenate(parts, axis=0)
    dq = dq + lax.dot_general(weights, p_ref[...], TN, preferred_element_type=F32)
    dp = jnp.dot(weights, q, preferred_element_type=F32)

    @pl.when(step == 0)
    def _():
        dp_v[...] = dp

    @pl.when(step > 0)
    def _():
        dp_v[...] += dp

    out_ref[...] = raw_gradient(raw_ref[...], inv_ref[:, k : k + 1], dq)

    @pl.when(step == lists - 1)
    def _():
        for at in range(0, rows, chunk):
            here = slice(at, at + chunk)
            part = raw_gradient(p_raw_ref[here, :], p_inv_ref[here, k : k + 1], dp_v[here, :])
            part_ref[here, :] = part.astype(BF16)


def passage_scratch(widths, far, rows, wide):
    return (
        [
            pltpu.VMEM((far, wide), BF16),
            pltpu.VMEM((rows, far), BF16),
            pltpu.VMEM((rows, LANES), F32),
            pltpu.VMEM((8, far), jnp.int32),
        ]
        + [pltpu.VMEM((rows, width), BF16) for width in widths]
        + [pltpu.VMEM((rows, width), F32) for width in widths]
        + [pltpu.SemaphoreType.DMA((4, 3)), pltpu.SemaphoreType.DMA((3, 4))]
    )


def passage_kernel(
    widths, starts, place_hbm, term_hbm, part0, part1, part2, inv_hbm,
    out0, out1, out2,
    term_v, pick_v, inv_ref, place_ref, pv0, pv1, pv2, ov0, ov1, ov2, in_sems, out_sems,
):
    parts, outs = (part0, part1, part2), (out0, out1, out2)
    part_vs, out_vs = (pv0, pv1, pv2), (ov0, ov1, ov2)
    rows = ov0.shape[0]
    far = term_v.shape[0]
    order = (0, 1, 2)
    chunk = min(256, rows)
    small = (
        pltpu.make_async_copy(place_hbm, place_ref, in_sems.at[3, 0]),
        pltpu.make_async_copy(inv_hbm, inv_ref, in_sems.at[3, 1]),
    )
    for load in small:
        load.start()
    loads = {}
    for k in order:
        span = pl.ds(starts[k], widths[k])
        loads[k] = (
            pltpu.make_async_copy(term_hbm.at[:, span], term_v.at[:, span], in_sems.at[k, 0]),
            pltpu.make_async_copy(parts[k], part_vs[k], in_sems.at[k, 1]),
        )
        for load in loads[k]:
            load.start()
    for load in small:
        load.wait()
    place = place_ref[0:1, :]
    for at in range(0, rows, chunk):
        row = lax.broadcasted_iota(jnp.int32, (chunk, far), 0) + at
        pick_v[at : at + chunk, :] = jnp.where(row == place, 1.0, 0.0).astype(BF16)
    stores = []
    for k in order:
        for load in loads[k]:
            load.wait()
        terms = term_v[:, starts[k] : starts[k] + widths[k]]
        for at in range(0, rows, chunk):
            here = slice(at, at + chunk)
            inverse = inv_ref[here, k : k + 1]
            added = jnp.dot(pick_v[here, :], terms, preferred_element_type=F32)
            added = added * inverse
            out_vs[k][here, :] = part_vs[k][here, :].astype(F32) + added
            part = pl.ds(at, chunk)
            store = pltpu.make_async_copy(
                out_vs[k].at[part, :], outs[k].at[part, :], out_sems.at[k, at // chunk]
            )
            store.start()
            stores.append(store)
    for store in stores:
        store.wait()


def local(
    query_first, query_second, query_third,
    passage_first, passage_second, passage_third,
    neg_blocks, positives,
):
    devices = lax.axis_size(AXES)
    own = lax.axis_index(AXES)
    queries = (query_first, query_second, query_third)
    passages = (passage_first, passage_second, passage_third)
    widths = [values.shape[1] for values in queries]
    starts = columns_of(widths)
    wide = sum(widths)
    rows = query_first.shape[0]
    block_count = rows // PROWS
    lists, entries = neg_blocks.shape
    far = devices * PROWS
    cols = rows // lists
    params = pltpu.CompilerParams(vmem_limit_bytes=62 * MIB)
    shape = jax.ShapeDtypeStruct

    wanted = pl.pallas_call(
        functools.partial(wanted_kernel, block_count),
        out_shape=jax.ShapeDtypeStruct((devices, LANES), jnp.int32),
        in_specs=[VMEM],
        out_specs=VMEM,
        compiler_params=params,
    )(neg_blocks)
    asked = exchange(wanted[:, None, :]).reshape(devices, LANES)

    step = rows // 4
    row_block = lambda width: pl.BlockSpec((step, width), lambda i: (i, 0))

    def heads(values, after):
        return pl.pallas_call(
            functools.partial(heads_kernel, widths, starts),
            grid=(4,),
            out_shape=(shape((rows, wide), BF16), shape((rows, LANES), F32)),
            in_specs=[row_block(width) for width in widths] + [HBM],
            out_specs=(row_block(wide), row_block(LANES)),
            compiler_params=params,
            cost_estimate=cost(rows * wide * 4, rows * wide * 4),
        )(*values, after)

    p_all, p_inverses = heads(passages, wanted)

    send = pl.pallas_call(
        gather_kernel,
        out_shape=shape((far, wide), BF16),
        in_specs=[SMEM, VMEM],
        out_specs=HBM,
        scratch_shapes=[pltpu.VMEM((far, wide), BF16), pltpu.SemaphoreType.DMA((8,))],
        compiler_params=params,
        cost_estimate=cost(far * wide, far * wide * 4),
    )(asked, p_all)
    fetched = exchange(send.reshape(devices, PROWS, wide)).reshape(far, wide)

    q_all, q_inverses = heads(queries, send)
    local_pos = (positives - own * rows).reshape(1, rows)
    whole = lambda dims: pl.BlockSpec(dims, lambda i: (0,) * len(dims))
    pos_block = pl.BlockSpec((1, cols), lambda i: (0, i))
    lane_block = pl.BlockSpec((8, cols), lambda i: (0, i))
    totals, positive_scores, bias, local_exps = pl.pallas_call(
        functools.partial(local_kernel, widths, starts, block_count),
        grid=(lists,),
        out_shape=(
            shape((8, rows), F32),
            shape((8, rows), F32),
            shape((far, LANES), F32),
            shape((3, rows, rows), BF16),
        ),
        in_specs=[
            whole((rows, wide)),
            pl.BlockSpec((cols, wide), lambda i: (i, 0)),
            pos_block,
            whole((lists, entries)),
        ],
        out_specs=(
            lane_block,
            lane_block,
            whole((far, LANES)),
            pl.BlockSpec((3, rows, cols), lambda i: (0, 0, i)),
        ),
        compiler_params=params,
        cost_estimate=cost(2 * rows * rows * wide, rows * wide * 4),
    )(p_all, q_all, local_pos, neg_blocks)

    terms, scales, loss_rows = pl.pallas_call(
        functools.partial(far_kernel, widths, starts, lists),
        out_shape=(shape((far, wide), BF16), shape((8, rows), F32), shape((8, rows), F32)),
        in_specs=[HBM] * 5,
        out_specs=(HBM,) * 3,
        scratch_shapes=far_scratch(far, rows, wide),
        compiler_params=params,
        cost_estimate=cost(4 * far * rows * wide, 6 * far * wide),
    )(fetched, q_all, bias, totals, positive_scores)
    losses = loss_rows[0] + loss_rows[1] + loss_rows[2]
    returned = exchange(terms.reshape(devices, PROWS, wide)).reshape(far, wide)

    q_grads = []
    p_parts = []
    for k in range(3):
        width = widths[k]
        place = starts[k] // width
        q_grad, p_part = pl.pallas_call(
            functools.partial(near_kernel, k, lists),
            grid=(lists,),
            out_shape=(shape((rows, width), F32), shape((rows, width), BF16)),
            in_specs=[
                pl.BlockSpec((rows, width), lambda i, place=place: (0, place)),
                pl.BlockSpec((cols, width), lambda i, place=place: (i, place)),
                pl.BlockSpec((far, width), lambda i, place=place: (0, place)),
                pl.BlockSpec((1, rows, cols), lambda i, k=k: (k, 0, i)),
                pl.BlockSpec((cols, width), lambda i: (i, 0)),
                pl.BlockSpec((cols, LANES), lambda i: (i, 0)),
                lane_block,
                whole((far, LANES)),
                pos_block,
                whole((rows, width)),
                whole((rows, LANES)),
            ],
            out_specs=(pl.BlockSpec((cols, width), lambda i: (i, 0)), whole((rows, width))),
            scratch_shapes=[pltpu.VMEM((rows, width), F32)],
            compiler_params=params,
            cost_estimate=cost(8 * rows * rows * width, 16 * rows * width),
        )(
            p_all, q_all, fetched, local_exps, queries[k], q_inverses, scales, bias, local_pos,
            passages[k], p_inverses,
        )
        q_grads.append(q_grad)
        p_parts.append(p_part)

    offsets = jnp.arange(PROWS, dtype=jnp.int32)
    asked_ids = asked[:, :1]
    place = jnp.where(asked_ids >= 0, asked_ids * PROWS + offsets[None, :], -1).reshape(1, far)
    place = jnp.broadcast_to(place, (8, far))
    p_grads = pl.pallas_call(
        functools.partial(passage_kernel, widths, starts),
        out_shape=tuple(shape((rows, width), F32) for width in widths),
        in_specs=[HBM] * 6,
        out_specs=(HBM,) * 3,
        scratch_shapes=passage_scratch(widths, far, rows, wide),
        compiler_params=params,
        cost_estimate=cost(16 * rows * wide, 12 * rows * wide),
    )(place, returned, *p_parts, p_inverses)
    return (losses, *q_grads, *p_grads)


def solution(mesh):
    rows = P(AXES, None)
    return jax.shard_map(
        local,
        mesh=mesh,
        in_specs=(rows,) * 7 + (P(AXES),),
        out_specs=(P(AXES),) + (rows,) * 6,
        check_vma=False,
    )
```

```python
import functools
import math

import jax
import jax.numpy as jnp
from jax import lax
from jax.experimental import pallas as pl
from jax.experimental.pallas import tpu as pltpu
from jax.sharding import PartitionSpec as P

PROWS = 8
LANES = 128
AXES = ("dp", "group")

EPSILON = 1e-06
SHARPNESS = 20.0
EXP_SCALE = SHARPNESS * math.log2(math.e)
OFF = -1e30

F32 = jnp.float32
BF16 = jnp.bfloat16
HBM = pl.BlockSpec(memory_space=pltpu.HBM)
VMEM = pl.BlockSpec(memory_space=pltpu.VMEM)
SMEM = pl.BlockSpec(memory_space=pltpu.SMEM)
MIB = 1024 * 1024
NT = (((1,), (1,)), ((), ()))
TN = (((0,), (0,)), ((), ()))
NN = (((1,), (0,)), ((), ()))


def exchange(values):
    return lax.all_to_all(values, AXES, split_axis=0, concat_axis=0, tiled=True)


def cost(flops, moved):
    return pl.CostEstimate(flops=int(flops), bytes_accessed=int(moved), transcendentals=0)


def columns_of(widths):
    starts = {}
    at = 0
    for index in sorted(range(len(widths)), key=lambda i: -widths[i]):
        starts[index] = at
        at += widths[index]
    return [starts[i] for i in range(len(widths))]


def wanted_kernel(block_count, neg_ref, out_ref):
    peers = out_ref.shape[0]
    lists, entries = neg_ref.shape
    peer = lax.broadcasted_iota(jnp.int32, (peers, entries), 0)
    best = jnp.full((peers, 1), -1, jnp.int32)
    for row in range(lists):
        ids = jnp.broadcast_to(neg_ref[row : row + 1, :], (peers, entries))
        local_ids = ids - peer * block_count
        hit = (local_ids >= 0) & (local_ids < block_count)
        best = jnp.maximum(best, jnp.max(jnp.where(hit, local_ids, -1), axis=1, keepdims=True))
    out_ref[...] = jnp.broadcast_to(best, out_ref.shape)


def heads_kernel(widths, starts, raw0, raw1, raw2, after_ref, out_ref, inv_ref):
    del after_ref
    lane = lax.broadcasted_iota(jnp.int32, inv_ref.shape, 1)
    packed = jnp.zeros(inv_ref.shape, F32)
    for k, raw in enumerate((raw0, raw1, raw2)):
        values = raw[...].astype(F32)
        inverse = lax.rsqrt(jnp.sum(values * values, axis=1, keepdims=True) + EPSILON)
        out_ref[:, starts[k] : starts[k] + widths[k]] = (values * inverse).astype(BF16)
        packed = jnp.where(lane == k, inverse, packed)
    inv_ref[...] = packed


def gather_kernel(widths, starts, asked_ref, raw0, raw1, raw2, out_hbm, out_v, sems):
    raws = (raw0, raw1, raw2)
    pairs = out_v.shape[0] // 16
    parts = min(8, pairs)
    each = pairs // parts

    def block(raw, peer):
        ident = jnp.maximum(asked_ref[peer, 0], 0)
        start = pl.multiple_of((ident // 2) * 16, 16)
        both = raw[pl.ds(start, 16), :].astype(F32)
        return jnp.where(ident % 2 == 0, both[:8], both[8:])

    stores = []
    for part in range(parts):
        for pair in range(part * each, (part + 1) * each):
            for k in range(3):
                values = jnp.concatenate([block(raws[k], pair * 2), block(raws[k], pair * 2 + 1)], axis=0)
                inverse = lax.rsqrt(jnp.sum(values * values, axis=1, keepdims=True) + EPSILON)
                place = slice(starts[k], starts[k] + widths[k])
                out_v[pair * 16 : pair * 16 + 16, place] = (values * inverse).astype(BF16)
        here = pl.ds(part * each * 16, each * 16)
        store = pltpu.make_async_copy(out_v.at[here, :], out_hbm.at[here, :], sems.at[part])
        store.start()
        stores.append(store)
    for store in stores:
        store.wait()


def local_kernel(
    widths, starts, block_count, p_ref, q_ref, pos_ref, neg_ref,
    tot_ref, spos_ref, bias_ref, e_ref,
):
    rows = p_ref.shape[0]
    cols = pos_ref.shape[1]
    chunk = min(256, rows)
    pos = pos_ref[0:1, :]
    for k in range(3):
        span = slice(starts[k], starts[k] + widths[k])
        q = q_ref[:, span]
        tot = jnp.zeros((1, cols), F32)
        spos = jnp.zeros((1, cols), F32)
        for at in range(0, rows, chunk):
            s = lax.dot_general(p_ref[at : at + chunk, span], q, NT, preferred_element_type=F32)
            row = lax.broadcasted_iota(jnp.int32, (chunk, cols), 0) + at
            e = jnp.exp2(s * EXP_SCALE)
            e_ref[k, at : at + chunk, :] = e.astype(BF16)
            tot = tot + jnp.sum(e, axis=0, keepdims=True)
            spos = spos + jnp.sum(jnp.where(row == pos, s, 0.0), axis=0, keepdims=True)
        tot_ref[k : k + 1, :] = tot
        spos_ref[k : k + 1, :] = spos * SHARPNESS
    @pl.when(pl.program_id(0) == 0)
    def _():
        far = bias_ref.shape[0]
        lists, entries = neg_ref.shape
        peer = lax.broadcasted_iota(jnp.int32, (far, entries), 0) // PROWS
        lane = lax.broadcasted_iota(jnp.int32, bias_ref.shape, 1)
        bias = jnp.full(bias_ref.shape, OFF, F32)
        for b in range(lists):
            local_ids = jnp.broadcast_to(neg_ref[b : b + 1, :], (far, entries)) - peer * block_count
            hit = (local_ids >= 0) & (local_ids < block_count)
            listed = jnp.max(jnp.where(hit, 1.0, 0.0), axis=1, keepdims=True)
            bias = jnp.where((lane == b) & (listed > 0.0), 0.0, bias)
        bias_ref[...] = bias


def far_scratch(far, rows, wide):
    return [
        pltpu.VMEM((far, wide), BF16),
        pltpu.VMEM((rows, wide), BF16),
        pltpu.VMEM((far, LANES), F32),
        pltpu.VMEM((8, rows), F32),
        pltpu.VMEM((8, rows), F32),
        pltpu.VMEM((8, rows), F32),
        pltpu.VMEM((8, rows), F32),
        pltpu.VMEM((far, rows), BF16),
        pltpu.VMEM((far, rows), F32),
        pltpu.VMEM((far, wide), BF16),
        pltpu.SemaphoreType.DMA((4, 3)),
        pltpu.SemaphoreType.DMA((4, 4)),
    ]


def far_kernel(
    widths, starts, lists, far_hbm, q_hbm, bias_hbm, tot_hbm, spos_hbm,
    term_hbm, scale_hbm, loss_hbm,
    far_ref, q_ref, bias_ref, tot_ref, spos_ref, scale_ref, loss_ref,
    g_ref, e_v, term_v, in_sems, out_sems,
):
    far, rows = g_ref.shape
    cols = rows // lists
    chunk = min(256, far)
    order = (0, 1, 2)
    loads = {}
    for k in order:
        span = pl.ds(starts[k], widths[k])
        loads[k] = [
            pltpu.make_async_copy(far_hbm.at[:, span], far_ref.at[:, span], in_sems.at[k, 0]),
            pltpu.make_async_copy(q_hbm.at[:, span], q_ref.at[:, span], in_sems.at[k, 1]),
        ]
        if k == order[0]:
            loads[k] += [
                pltpu.make_async_copy(bias_hbm, bias_ref, in_sems.at[3, 0]),
                pltpu.make_async_copy(tot_hbm, tot_ref, in_sems.at[3, 1]),
                pltpu.make_async_copy(spos_hbm, spos_ref, in_sems.at[3, 2]),
            ]
        for load in loads[k]:
            load.start()
    scale_ref[3:8, :] = jnp.zeros((5, rows), F32)
    loss_ref[3:8, :] = jnp.zeros((5, rows), F32)
    stores = []
    for k in order:
        span = slice(starts[k], starts[k] + widths[k])
        for load in loads[k]:
            load.wait()
        for b in range(lists):
            at_q = slice(b * cols, (b + 1) * cols)
            q = q_ref[at_q, span]
            tot = tot_ref[k : k + 1, at_q]
            for at in range(0, far, chunk):
                s = lax.dot_general(far_ref[at : at + chunk, span], q, NT, preferred_element_type=F32)
                bias = bias_ref[at : at + chunk, b : b + 1]
                e = jnp.exp2(s * EXP_SCALE + bias)
                tot = tot + jnp.sum(e, axis=0, keepdims=True)
                e_v[at : at + chunk, at_q] = e
            scale = SHARPNESS / tot
            scale_ref[k : k + 1, at_q] = scale
            loss_ref[k : k + 1, at_q] = jnp.log(tot) - spos_ref[k : k + 1, at_q]
            for at in range(0, far, chunk):
                g_ref[at : at + chunk, at_q] = (e_v[at : at + chunk, at_q] * scale).astype(BF16)
        if k == order[-1]:
            for index, (ref, hbm) in enumerate(((scale_ref, scale_hbm), (loss_ref, loss_hbm))):
                stores.append(pltpu.make_async_copy(ref, hbm, out_sems.at[3, index]))
                stores[-1].start()
        for row in range(0, far, chunk):
            here = slice(row, row + chunk)
            part = jnp.dot(g_ref[here, :], q_ref[:, span], preferred_element_type=F32)
            unit = far_ref[here, span].astype(F32)
            part = part - unit * jnp.sum(unit * part, axis=1, keepdims=True)
            term_v[here, span] = part.astype(BF16)
            place = (pl.ds(row, chunk), pl.ds(starts[k], widths[k]))
            store = pltpu.make_async_copy(
                term_v.at[place], term_hbm.at[place], out_sems.at[k, row // chunk]
            )
            store.start()
            stores.append(store)
    for store in stores:
        store.wait()


def raw_gradient(raw, inverse, grad):
    unit = raw.astype(F32) * inverse
    return (grad - unit * jnp.sum(unit * grad, axis=1, keepdims=True)) * inverse


def near_kernel(
    k, lists, p_ref, q_ref, far_ref, e_ref, raw_ref, inv_ref, scale_ref, bias_ref, pos_ref,
    p_raw_ref, p_inv_ref, out_ref, part_ref, dp_v,
):
    rows = p_ref.shape[0]
    far = far_ref.shape[0]
    cols = q_ref.shape[0]
    q = q_ref[...]
    pos = pos_ref[0:1, :]
    scale = scale_ref[k : k + 1, :]
    chunk = min(256, rows, far)
    step = pl.program_id(0)
    lane = lax.broadcasted_iota(jnp.int32, (chunk, LANES), 1)
    parts = []
    for at in range(0, far, chunk):
        s = lax.dot_general(far_ref[at : at + chunk, :], q, NT, preferred_element_type=F32)
        bias = jnp.sum(jnp.where(lane == step, bias_ref[at : at + chunk, :], 0.0), axis=1, keepdims=True)
        parts.append((jnp.exp2(s * EXP_SCALE + bias) * scale).astype(BF16))
    dq = lax.dot_general(
        jnp.concatenate(parts, axis=0), far_ref[...], TN, preferred_element_type=F32
    )
    parts = []
    for at in range(0, rows, chunk):
        row = lax.broadcasted_iota(jnp.int32, (chunk, cols), 0) + at
        g = e_ref[0, at : at + chunk, :].astype(F32) * scale
        parts.append((g - jnp.where(row == pos, SHARPNESS, 0.0)).astype(BF16))
    weights = jnp.concatenate(parts, axis=0)
    dq = dq + lax.dot_general(weights, p_ref[...], TN, preferred_element_type=F32)
    dp = jnp.dot(weights, q, preferred_element_type=F32)

    @pl.when(step == 0)
    def _():
        dp_v[...] = dp

    @pl.when(step > 0)
    def _():
        dp_v[...] += dp

    out_ref[...] = raw_gradient(raw_ref[...], inv_ref[:, k : k + 1], dq)

    @pl.when(step == lists - 1)
    def _():
        for at in range(0, rows, chunk):
            here = slice(at, at + chunk)
            part = raw_gradient(p_raw_ref[here, :], p_inv_ref[here, k : k + 1], dp_v[here, :])
            part_ref[here, :] = part.astype(BF16)


def passage_scratch(widths, far, rows, wide):
    return (
        [
            pltpu.VMEM((far, wide), BF16),
            pltpu.VMEM((rows, far), BF16),
            pltpu.VMEM((rows, LANES), F32),
            pltpu.VMEM((1, far), jnp.int32),
        ]
        + [pltpu.VMEM((rows, width), BF16) for width in widths]
        + [pltpu.VMEM((rows, width), F32) for width in widths]
        + [pltpu.SemaphoreType.DMA((4, 3)), pltpu.SemaphoreType.DMA((3, 4))]
    )


def passage_kernel(
    widths, starts, place_hbm, term_hbm, part0, part1, part2, inv_hbm,
    out0, out1, out2,
    term_v, pick_v, inv_ref, place_ref, pv0, pv1, pv2, ov0, ov1, ov2, in_sems, out_sems,
):
    parts, outs = (part0, part1, part2), (out0, out1, out2)
    part_vs, out_vs = (pv0, pv1, pv2), (ov0, ov1, ov2)
    rows = ov0.shape[0]
    far = term_v.shape[0]
    order = (0, 1, 2)
    chunk = min(256, rows)
    small = (
        pltpu.make_async_copy(place_hbm, place_ref, in_sems.at[3, 0]),
        pltpu.make_async_copy(inv_hbm, inv_ref, in_sems.at[3, 1]),
    )
    for load in small:
        load.start()
    loads = {}
    for k in order:
        span = pl.ds(starts[k], widths[k])
        loads[k] = (
            pltpu.make_async_copy(term_hbm.at[:, span], term_v.at[:, span], in_sems.at[k, 0]),
            pltpu.make_async_copy(parts[k], part_vs[k], in_sems.at[k, 1]),
        )
        for load in loads[k]:
            load.start()
    for load in small:
        load.wait()
    place = place_ref[...]
    for at in range(0, rows, chunk):
        row = lax.broadcasted_iota(jnp.int32, (chunk, far), 0) + at
        pick_v[at : at + chunk, :] = jnp.where(row == place, 1.0, 0.0).astype(BF16)
    stores = []
    for k in order:
        for load in loads[k]:
            load.wait()
        terms = term_v[:, starts[k] : starts[k] + widths[k]]
        for at in range(0, rows, chunk):
            here = slice(at, at + chunk)
            inverse = inv_ref[here, k : k + 1]
            added = jnp.dot(pick_v[here, :], terms, preferred_element_type=F32)
            added = added * inverse
            out_vs[k][here, :] = part_vs[k][here, :].astype(F32) + added
            part = pl.ds(at, chunk)
            store = pltpu.make_async_copy(
                out_vs[k].at[part, :], outs[k].at[part, :], out_sems.at[k, at // chunk]
            )
            store.start()
            stores.append(store)
    for store in stores:
        store.wait()


def local(
    query_first, query_second, query_third,
    passage_first, passage_second, passage_third,
    neg_blocks, positives,
):
    devices = lax.axis_size(AXES)
    own = lax.axis_index(AXES)
    queries = (query_first, query_second, query_third)
    passages = (passage_first, passage_second, passage_third)
    widths = [values.shape[1] for values in queries]
    starts = columns_of(widths)
    wide = sum(widths)
    rows = query_first.shape[0]
    block_count = rows // PROWS
    lists, entries = neg_blocks.shape
    far = devices * PROWS
    cols = rows // lists
    params = pltpu.CompilerParams(vmem_limit_bytes=62 * MIB)
    shape = jax.ShapeDtypeStruct

    wanted = pl.pallas_call(
        functools.partial(wanted_kernel, block_count),
        out_shape=jax.ShapeDtypeStruct((devices, LANES), jnp.int32),
        in_specs=[VMEM],
        out_specs=VMEM,
        compiler_params=params,
    )(neg_blocks)
    asked = exchange(wanted[:, None, :]).reshape(devices, LANES)

    step = rows // 4
    row_block = lambda width: pl.BlockSpec((step, width), lambda i: (i, 0))

    def heads(values, after):
        return pl.pallas_call(
            functools.partial(heads_kernel, widths, starts),
            grid=(4,),
            out_shape=(shape((rows, wide), BF16), shape((rows, LANES), F32)),
            in_specs=[row_block(width) for width in widths] + [HBM],
            out_specs=(row_block(wide), row_block(LANES)),
            compiler_params=params,
            cost_estimate=cost(rows * wide * 4, rows * wide * 4),
        )(*values, after)

    send = pl.pallas_call(
        functools.partial(gather_kernel, widths, starts),
        out_shape=shape((far, wide), BF16),
        in_specs=[SMEM, VMEM, VMEM, VMEM],
        out_specs=HBM,
        scratch_shapes=[pltpu.VMEM((far, wide), BF16), pltpu.SemaphoreType.DMA((8,))],
        compiler_params=pltpu.CompilerParams(vmem_limit_bytes=62 * MIB),
        cost_estimate=cost(far * wide * 4, far * wide * 4),
    )(asked, *passages)
    fetched = exchange(send.reshape(devices, PROWS, wide)).reshape(far, wide)

    p_all, p_inverses = heads(passages, send)
    q_all, q_inverses = heads(queries, send)
    local_pos = (positives - own * rows).reshape(1, rows)
    whole = lambda dims: pl.BlockSpec(dims, lambda i: (0,) * len(dims))
    pos_block = pl.BlockSpec((1, cols), lambda i: (0, i))
    lane_block = pl.BlockSpec((8, cols), lambda i: (0, i))
    totals, positive_scores, bias, local_exps = pl.pallas_call(
        functools.partial(local_kernel, widths, starts, block_count),
        grid=(lists,),
        out_shape=(
            shape((8, rows), F32),
            shape((8, rows), F32),
            shape((far, LANES), F32),
            shape((3, rows, rows), BF16),
        ),
        in_specs=[
            whole((rows, wide)),
            pl.BlockSpec((cols, wide), lambda i: (i, 0)),
            pos_block,
            whole((lists, entries)),
        ],
        out_specs=(
            lane_block,
            lane_block,
            whole((far, LANES)),
            pl.BlockSpec((3, rows, cols), lambda i: (0, 0, i)),
        ),
        compiler_params=params,
        cost_estimate=cost(2 * rows * rows * wide, rows * wide * 4),
    )(p_all, q_all, local_pos, neg_blocks)

    terms, scales, loss_rows = pl.pallas_call(
        functools.partial(far_kernel, widths, starts, lists),
        out_shape=(shape((far, wide), BF16), shape((8, rows), F32), shape((8, rows), F32)),
        in_specs=[HBM] * 5,
        out_specs=(HBM,) * 3,
        scratch_shapes=far_scratch(far, rows, wide),
        compiler_params=params,
        cost_estimate=cost(4 * far * rows * wide, 6 * far * wide),
    )(fetched, q_all, bias, totals, positive_scores)
    losses = loss_rows[0] + loss_rows[1] + loss_rows[2]
    returned = exchange(terms.reshape(devices, PROWS, wide)).reshape(far, wide)

    q_grads = []
    p_parts = []
    for k in range(3):
        width = widths[k]
        place = starts[k] // width
        q_grad, p_part = pl.pallas_call(
            functools.partial(near_kernel, k, lists),
            grid=(lists,),
            out_shape=(shape((rows, width), F32), shape((rows, width), BF16)),
            in_specs=[
                pl.BlockSpec((rows, width), lambda i, place=place: (0, place)),
                pl.BlockSpec((cols, width), lambda i, place=place: (i, place)),
                pl.BlockSpec((far, width), lambda i, place=place: (0, place)),
                pl.BlockSpec((1, rows, cols), lambda i, k=k: (k, 0, i)),
                pl.BlockSpec((cols, width), lambda i: (i, 0)),
                pl.BlockSpec((cols, LANES), lambda i: (i, 0)),
                lane_block,
                whole((far, LANES)),
                pos_block,
                whole((rows, width)),
                whole((rows, LANES)),
            ],
            out_specs=(pl.BlockSpec((cols, width), lambda i: (i, 0)), whole((rows, width))),
            scratch_shapes=[pltpu.VMEM((rows, width), F32)],
            compiler_params=params,
            cost_estimate=cost(8 * rows * rows * width, 16 * rows * width),
        )(
            p_all, q_all, fetched, local_exps, queries[k], q_inverses, scales, bias, local_pos,
            passages[k], p_inverses,
        )
        q_grads.append(q_grad)
        p_parts.append(p_part)

    offsets = jnp.arange(PROWS, dtype=jnp.int32)
    asked_ids = asked[:, :1]
    place = jnp.where(asked_ids >= 0, asked_ids * PROWS + offsets[None, :], -1).reshape(1, far)
    p_grads = pl.pallas_call(
        functools.partial(passage_kernel, widths, starts),
        out_shape=tuple(shape((rows, width), F32) for width in widths),
        in_specs=[HBM] * 6,
        out_specs=(HBM,) * 3,
        scratch_shapes=passage_scratch(widths, far, rows, wide),
        compiler_params=params,
        cost_estimate=cost(16 * rows * wide, 12 * rows * wide),
    )(place, returned, *p_parts, p_inverses)
    return (losses, *q_grads, *p_grads)


def solution(mesh):
    rows = P(AXES, None)
    return jax.shard_map(
        local,
        mesh=mesh,
        in_specs=(rows,) * 7 + (P(AXES),),
        out_specs=(P(AXES),) + (rows,) * 6,
        check_vma=False,
    )
```

```python
import functools
import math

import jax
import jax.numpy as jnp
from jax import lax
from jax.experimental import pallas as pl
from jax.experimental.pallas import tpu as pltpu
from jax.sharding import PartitionSpec as P

PROWS = 8
LANES = 128
AXES = ("dp", "group")

EPSILON = 1e-06
SHARPNESS = 20.0
EXP_SCALE = SHARPNESS * math.log2(math.e)
OFF = -1e30

F32 = jnp.float32
BF16 = jnp.bfloat16
HBM = pl.BlockSpec(memory_space=pltpu.HBM)
VMEM = pl.BlockSpec(memory_space=pltpu.VMEM)
SMEM = pl.BlockSpec(memory_space=pltpu.SMEM)
MIB = 1024 * 1024
NT = (((1,), (1,)), ((), ()))
TN = (((0,), (0,)), ((), ()))
NN = (((1,), (0,)), ((), ()))


def exchange(values):
    return lax.all_to_all(values, AXES, split_axis=0, concat_axis=0, tiled=True)


def cost(flops, moved):
    return pl.CostEstimate(flops=int(flops), bytes_accessed=int(moved), transcendentals=0)


def columns_of(widths):
    starts = {}
    at = 0
    for index in sorted(range(len(widths)), key=lambda i: -widths[i]):
        starts[index] = at
        at += widths[index]
    return [starts[i] for i in range(len(widths))]


def wanted_kernel(block_count, neg_ref, out_ref):
    peers = out_ref.shape[0]
    lists, entries = neg_ref.shape
    peer = lax.broadcasted_iota(jnp.int32, (peers, entries), 0)
    best = jnp.full((peers, entries), -1, jnp.int32)
    for row in range(lists):
        ids = jnp.broadcast_to(neg_ref[row : row + 1, :], (peers, entries))
        local_ids = ids - peer * block_count
        hit = (local_ids >= 0) & (local_ids < block_count)
        best = jnp.maximum(best, jnp.where(hit, local_ids, -1))
    best = jnp.max(best.astype(F32), axis=1, keepdims=True)
    out_ref[...] = jnp.broadcast_to(best, out_ref.shape).astype(jnp.int32)


def heads_kernel(widths, starts, raw0, raw1, raw2, after_ref, out_ref, inv_ref):
    del after_ref
    lane = lax.broadcasted_iota(jnp.int32, inv_ref.shape, 1)
    packed = jnp.zeros(inv_ref.shape, F32)
    for k, raw in enumerate((raw0, raw1, raw2)):
        values = raw[...].astype(F32)
        inverse = lax.rsqrt(jnp.sum(values * values, axis=1, keepdims=True) + EPSILON)
        out_ref[:, starts[k] : starts[k] + widths[k]] = (values * inverse).astype(BF16)
        packed = jnp.where(lane == k, inverse, packed)
    inv_ref[...] = packed


def gather_kernel(widths, starts, asked_ref, raw0, raw1, raw2, out_hbm, out_v, sems):
    raws = (raw0, raw1, raw2)
    pairs = out_v.shape[0] // 16
    parts = min(8, pairs)
    each = pairs // parts

    def block(raw, peer):
        ident = jnp.maximum(asked_ref[peer, 0], 0)
        start = pl.multiple_of((ident // 2) * 16, 16)
        both = raw[pl.ds(start, 16), :].astype(F32)
        return jnp.where(ident % 2 == 0, both[:8], both[8:])

    stores = []
    for part in range(parts):
        for pair in range(part * each, (part + 1) * each):
            for k in range(3):
                values = jnp.concatenate([block(raws[k], pair * 2), block(raws[k], pair * 2 + 1)], axis=0)
                inverse = lax.rsqrt(jnp.sum(values * values, axis=1, keepdims=True) + EPSILON)
                place = slice(starts[k], starts[k] + widths[k])
                out_v[pair * 16 : pair * 16 + 16, place] = (values * inverse).astype(BF16)
        here = pl.ds(part * each * 16, each * 16)
        store = pltpu.make_async_copy(out_v.at[here, :], out_hbm.at[here, :], sems.at[part])
        store.start()
        stores.append(store)
    for store in stores:
        store.wait()


def local_kernel(
    widths, starts, block_count, p_ref, q_ref, pos_ref, neg_ref,
    tot_ref, spos_ref, bias_ref, e_ref,
):
    rows = p_ref.shape[0]
    cols = pos_ref.shape[1]
    chunk = min(256, rows)
    pos = pos_ref[0:1, :]
    for k in range(3):
        span = slice(starts[k], starts[k] + widths[k])
        q = q_ref[:, span]
        tot = jnp.zeros((1, cols), F32)
        spos = jnp.zeros((1, cols), F32)
        for at in range(0, rows, chunk):
            s = lax.dot_general(p_ref[at : at + chunk, span], q, NT, preferred_element_type=F32)
            row = lax.broadcasted_iota(jnp.int32, (chunk, cols), 0) + at
            e = jnp.exp2(s * EXP_SCALE)
            e_ref[k, at : at + chunk, :] = e.astype(BF16)
            tot = tot + jnp.sum(e, axis=0, keepdims=True)
            spos = spos + jnp.sum(jnp.where(row == pos, s, 0.0), axis=0, keepdims=True)
        tot_ref[k : k + 1, :] = tot
        spos_ref[k : k + 1, :] = spos * SHARPNESS
    @pl.when(pl.program_id(0) == 0)
    def _():
        far = bias_ref.shape[0]
        lists, entries = neg_ref.shape
        peer = lax.broadcasted_iota(jnp.int32, (far, entries), 0) // PROWS
        lane = lax.broadcasted_iota(jnp.int32, bias_ref.shape, 1)
        bias = jnp.full(bias_ref.shape, OFF, F32)
        for b in range(lists):
            local_ids = jnp.broadcast_to(neg_ref[b : b + 1, :], (far, entries)) - peer * block_count
            hit = (local_ids >= 0) & (local_ids < block_count)
            listed = jnp.max(jnp.where(hit, 1.0, 0.0), axis=1, keepdims=True)
            bias = jnp.where((lane == b) & (listed > 0.0), 0.0, bias)
        bias_ref[...] = bias


def far_scratch(far, rows, wide):
    return [
        pltpu.VMEM((far, wide), BF16),
        pltpu.VMEM((rows, wide), BF16),
        pltpu.VMEM((far, LANES), F32),
        pltpu.VMEM((8, rows), F32),
        pltpu.VMEM((8, rows), F32),
        pltpu.VMEM((8, rows), F32),
        pltpu.VMEM((8, rows), F32),
        pltpu.VMEM((3, far, rows), BF16),
        pltpu.VMEM((2, far, rows), F32),
        pltpu.VMEM((far, wide), BF16),
        pltpu.SemaphoreType.DMA((4, 3)),
        pltpu.SemaphoreType.DMA((4, 4)),
    ]


def far_kernel(
    widths, starts, lists, far_hbm, q_hbm, bias_hbm, tot_hbm, spos_hbm,
    term_hbm, scale_hbm, loss_hbm,
    far_ref, q_ref, bias_ref, tot_ref, spos_ref, scale_ref, loss_ref,
    g_ref, e_v, term_v, in_sems, out_sems,
):
    far, rows = g_ref.shape[1:]
    cols = rows // lists
    chunk = min(256, far)
    order = (0, 1, 2)
    loads = {}
    for k in order:
        span = pl.ds(starts[k], widths[k])
        loads[k] = [
            pltpu.make_async_copy(far_hbm.at[:, span], far_ref.at[:, span], in_sems.at[k, 0]),
            pltpu.make_async_copy(q_hbm.at[:, span], q_ref.at[:, span], in_sems.at[k, 1]),
        ]
        if k == order[0]:
            loads[k] += [
                pltpu.make_async_copy(bias_hbm, bias_ref, in_sems.at[3, 0]),
                pltpu.make_async_copy(tot_hbm, tot_ref, in_sems.at[3, 1]),
                pltpu.make_async_copy(spos_hbm, spos_ref, in_sems.at[3, 2]),
            ]
        for load in loads[k]:
            load.start()
    scale_ref[3:8, :] = jnp.zeros((5, rows), F32)
    loss_ref[3:8, :] = jnp.zeros((5, rows), F32)
    stores = []
    def scores(k):
        span = slice(starts[k], starts[k] + widths[k])
        for load in loads[k]:
            load.wait()
        for b in range(lists):
            at_q = slice(b * cols, (b + 1) * cols)
            q = q_ref[at_q, span]
            tot = tot_ref[k : k + 1, at_q]
            for at in range(0, far, chunk):
                s = lax.dot_general(far_ref[at : at + chunk, span], q, NT, preferred_element_type=F32)
                bias = bias_ref[at : at + chunk, b : b + 1]
                e = jnp.exp2(s * EXP_SCALE + bias)
                tot = tot + jnp.sum(e, axis=0, keepdims=True)
                e_v[k % 2, at : at + chunk, at_q] = e
            scale = SHARPNESS / tot
            scale_ref[k : k + 1, at_q] = scale
            loss_ref[k : k + 1, at_q] = jnp.log(tot) - spos_ref[k : k + 1, at_q]
            for at in range(0, far, chunk):
                g_ref[k, at : at + chunk, at_q] = (e_v[k % 2, at : at + chunk, at_q] * scale).astype(BF16)

    def send(k):
        span = slice(starts[k], starts[k] + widths[k])
        for row in range(0, far, chunk):
            here = slice(row, row + chunk)
            part = jnp.dot(g_ref[k, here, :], q_ref[:, span], preferred_element_type=F32)
            unit = far_ref[here, span].astype(F32)
            part = part - unit * jnp.sum(unit * part, axis=1, keepdims=True)
            term_v[here, span] = part.astype(BF16)
            place = (pl.ds(row, chunk), pl.ds(starts[k], widths[k]))
            store = pltpu.make_async_copy(
                term_v.at[place], term_hbm.at[place], out_sems.at[k, row // chunk]
            )
            store.start()
            stores.append(store)

    scores(order[0])
    send(order[0])
    scores(order[1])
    send(order[1])
    scores(order[2])
    for index, (ref, hbm) in enumerate(((scale_ref, scale_hbm), (loss_ref, loss_hbm))):
        stores.append(pltpu.make_async_copy(ref, hbm, out_sems.at[3, index]))
        stores[-1].start()
    send(order[2])
    for store in stores:
        store.wait()


def raw_gradient(raw, inverse, grad):
    unit = raw.astype(F32) * inverse
    return (grad - unit * jnp.sum(unit * grad, axis=1, keepdims=True)) * inverse


def near_kernel(
    k, lists, p_ref, q_ref, far_ref, e_ref, raw_ref, inv_ref, scale_ref, bias_ref, pos_ref,
    p_raw_ref, p_inv_ref, out_ref, part_ref, dp_v,
):
    rows = p_ref.shape[0]
    far = far_ref.shape[0]
    cols = q_ref.shape[0]
    q = q_ref[...]
    pos = pos_ref[0:1, :]
    scale = scale_ref[k : k + 1, :]
    chunk = min(256, rows, far)
    step = pl.program_id(0)
    lane = lax.broadcasted_iota(jnp.int32, (chunk, LANES), 1)
    parts = []
    for at in range(0, far, chunk):
        s = lax.dot_general(far_ref[at : at + chunk, :], q, NT, preferred_element_type=F32)
        bias = jnp.sum(jnp.where(lane == step, bias_ref[at : at + chunk, :], 0.0), axis=1, keepdims=True)
        parts.append((jnp.exp2(s * EXP_SCALE + bias) * scale).astype(BF16))
    dq = lax.dot_general(
        jnp.concatenate(parts, axis=0), far_ref[...], TN, preferred_element_type=F32
    )
    parts = []
    for at in range(0, rows, chunk):
        row = lax.broadcasted_iota(jnp.int32, (chunk, cols), 0) + at
        g = e_ref[0, at : at + chunk, :].astype(F32) * scale
        parts.append((g - jnp.where(row == pos, SHARPNESS, 0.0)).astype(BF16))
    weights = jnp.concatenate(parts, axis=0)
    dq = dq + lax.dot_general(weights, p_ref[...], TN, preferred_element_type=F32)
    dp = jnp.dot(weights, q, preferred_element_type=F32)

    @pl.when(step == 0)
    def _():
        dp_v[...] = dp

    @pl.when(step > 0)
    def _():
        dp_v[...] += dp

    out_ref[...] = raw_gradient(raw_ref[...], inv_ref[:, k : k + 1], dq)

    @pl.when(step == lists - 1)
    def _():
        for at in range(0, rows, chunk):
            here = slice(at, at + chunk)
            part = raw_gradient(p_raw_ref[here, :], p_inv_ref[here, k : k + 1], dp_v[here, :])
            part_ref[here, :] = part.astype(BF16)


def passage_scratch(widths, far, rows, wide):
    return (
        [
            pltpu.VMEM((far, wide), BF16),
            pltpu.VMEM((rows, far), BF16),
            pltpu.VMEM((rows, LANES), F32),
            pltpu.VMEM((1, far), jnp.int32),
        ]
        + [pltpu.VMEM((rows, width), BF16) for width in widths]
        + [pltpu.VMEM((rows, width), F32) for width in widths]
        + [pltpu.SemaphoreType.DMA((4, 3)), pltpu.SemaphoreType.DMA((3, 4))]
    )


def passage_kernel(
    widths, starts, place_hbm, term_hbm, part0, part1, part2, inv_hbm,
    out0, out1, out2,
    term_v, pick_v, inv_ref, place_ref, pv0, pv1, pv2, ov0, ov1, ov2, in_sems, out_sems,
):
    parts, outs = (part0, part1, part2), (out0, out1, out2)
    part_vs, out_vs = (pv0, pv1, pv2), (ov0, ov1, ov2)
    rows = ov0.shape[0]
    far = term_v.shape[0]
    order = (0, 1, 2)
    chunk = min(256, rows)
    small = (
        pltpu.make_async_copy(place_hbm, place_ref, in_sems.at[3, 0]),
        pltpu.make_async_copy(inv_hbm, inv_ref, in_sems.at[3, 1]),
    )
    for load in small:
        load.start()
    loads = {}
    for k in order:
        span = pl.ds(starts[k], widths[k])
        loads[k] = (
            pltpu.make_async_copy(term_hbm.at[:, span], term_v.at[:, span], in_sems.at[k, 0]),
            pltpu.make_async_copy(parts[k], part_vs[k], in_sems.at[k, 1]),
        )
        for load in loads[k]:
            load.start()
    for load in small:
        load.wait()
    place = place_ref[...]
    for at in range(0, rows, chunk):
        row = lax.broadcasted_iota(jnp.int32, (chunk, far), 0) + at
        pick_v[at : at + chunk, :] = jnp.where(row == place, 1.0, 0.0).astype(BF16)
    stores = []
    for k in order:
        for load in loads[k]:
            load.wait()
        terms = term_v[:, starts[k] : starts[k] + widths[k]]
        for at in range(0, rows, chunk):
            here = slice(at, at + chunk)
            inverse = inv_ref[here, k : k + 1]
            added = jnp.dot(pick_v[here, :], terms, preferred_element_type=F32)
            added = added * inverse
            out_vs[k][here, :] = part_vs[k][here, :].astype(F32) + added
            part = pl.ds(at, chunk)
            store = pltpu.make_async_copy(
                out_vs[k].at[part, :], outs[k].at[part, :], out_sems.at[k, at // chunk]
            )
            store.start()
            stores.append(store)
    for store in stores:
        store.wait()


def local(
    query_first, query_second, query_third,
    passage_first, passage_second, passage_third,
    neg_blocks, positives,
):
    devices = lax.axis_size(AXES)
    own = lax.axis_index(AXES)
    queries = (query_first, query_second, query_third)
    passages = (passage_first, passage_second, passage_third)
    widths = [values.shape[1] for values in queries]
    starts = columns_of(widths)
    wide = sum(widths)
    rows = query_first.shape[0]
    block_count = rows // PROWS
    lists, entries = neg_blocks.shape
    far = devices * PROWS
    cols = rows // lists
    params = pltpu.CompilerParams(vmem_limit_bytes=62 * MIB)
    shape = jax.ShapeDtypeStruct

    wanted = pl.pallas_call(
        functools.partial(wanted_kernel, block_count),
        out_shape=jax.ShapeDtypeStruct((devices, LANES), jnp.int32),
        in_specs=[VMEM],
        out_specs=VMEM,
        compiler_params=params,
    )(neg_blocks)
    asked = exchange(wanted[:, None, :]).reshape(devices, LANES)

    step = rows // 4
    row_block = lambda width: pl.BlockSpec((step, width), lambda i: (i, 0))

    def heads(values, after):
        return pl.pallas_call(
            functools.partial(heads_kernel, widths, starts),
            grid=(4,),
            out_shape=(shape((rows, wide), BF16), shape((rows, LANES), F32)),
            in_specs=[row_block(width) for width in widths] + [HBM],
            out_specs=(row_block(wide), row_block(LANES)),
            compiler_params=params,
            cost_estimate=cost(rows * wide * 4, rows * wide * 4),
        )(*values, after)

    send = pl.pallas_call(
        functools.partial(gather_kernel, widths, starts),
        out_shape=shape((far, wide), BF16),
        in_specs=[SMEM, VMEM, VMEM, VMEM],
        out_specs=HBM,
        scratch_shapes=[pltpu.VMEM((far, wide), BF16), pltpu.SemaphoreType.DMA((8,))],
        compiler_params=pltpu.CompilerParams(vmem_limit_bytes=62 * MIB),
        cost_estimate=cost(far * wide * 4, far * wide * 4),
    )(asked, *passages)
    fetched = exchange(send.reshape(devices, PROWS, wide)).reshape(far, wide)

    p_all, p_inverses = heads(passages, send)
    q_all, q_inverses = heads(queries, send)
    local_pos = (positives - own * rows).reshape(1, rows)
    whole = lambda dims: pl.BlockSpec(dims, lambda i: (0,) * len(dims))
    pos_block = pl.BlockSpec((1, cols), lambda i: (0, i))
    lane_block = pl.BlockSpec((8, cols), lambda i: (0, i))
    totals, positive_scores, bias, local_exps = pl.pallas_call(
        functools.partial(local_kernel, widths, starts, block_count),
        grid=(lists,),
        out_shape=(
            shape((8, rows), F32),
            shape((8, rows), F32),
            shape((far, LANES), F32),
            shape((3, rows, rows), BF16),
        ),
        in_specs=[
            whole((rows, wide)),
            pl.BlockSpec((cols, wide), lambda i: (i, 0)),
            pos_block,
            whole((lists, entries)),
        ],
        out_specs=(
            lane_block,
            lane_block,
            whole((far, LANES)),
            pl.BlockSpec((3, rows, cols), lambda i: (0, 0, i)),
        ),
        compiler_params=params,
        cost_estimate=cost(2 * rows * rows * wide, rows * wide * 4),
    )(p_all, q_all, local_pos, neg_blocks)

    terms, scales, loss_rows = pl.pallas_call(
        functools.partial(far_kernel, widths, starts, lists),
        out_shape=(shape((far, wide), BF16), shape((8, rows), F32), shape((8, rows), F32)),
        in_specs=[HBM] * 5,
        out_specs=(HBM,) * 3,
        scratch_shapes=far_scratch(far, rows, wide),
        compiler_params=params,
        cost_estimate=cost(4 * far * rows * wide, 6 * far * wide),
    )(fetched, q_all, bias, totals, positive_scores)
    losses = loss_rows[0] + loss_rows[1] + loss_rows[2]
    returned = exchange(terms.reshape(devices, PROWS, wide)).reshape(far, wide)

    q_grads = []
    p_parts = []
    for k in range(3):
        width = widths[k]
        place = starts[k] // width
        q_grad, p_part = pl.pallas_call(
            functools.partial(near_kernel, k, lists),
            grid=(lists,),
            out_shape=(shape((rows, width), F32), shape((rows, width), BF16)),
            in_specs=[
                pl.BlockSpec((rows, width), lambda i, place=place: (0, place)),
                pl.BlockSpec((cols, width), lambda i, place=place: (i, place)),
                pl.BlockSpec((far, width), lambda i, place=place: (0, place)),
                pl.BlockSpec((1, rows, cols), lambda i, k=k: (k, 0, i)),
                pl.BlockSpec((cols, width), lambda i: (i, 0)),
                pl.BlockSpec((cols, LANES), lambda i: (i, 0)),
                lane_block,
                whole((far, LANES)),
                pos_block,
                whole((rows, width)),
                whole((rows, LANES)),
            ],
            out_specs=(pl.BlockSpec((cols, width), lambda i: (i, 0)), whole((rows, width))),
            scratch_shapes=[pltpu.VMEM((rows, width), F32)],
            compiler_params=params,
            cost_estimate=cost(8 * rows * rows * width, 16 * rows * width),
        )(
            p_all, q_all, fetched, local_exps, queries[k], q_inverses, scales, bias, local_pos,
            passages[k], p_inverses,
        )
        q_grads.append(q_grad)
        p_parts.append(p_part)

    offsets = jnp.arange(PROWS, dtype=jnp.int32)
    asked_ids = asked[:, :1]
    place = jnp.where(asked_ids >= 0, asked_ids * PROWS + offsets[None, :], -1).reshape(1, far)
    p_grads = pl.pallas_call(
        functools.partial(passage_kernel, widths, starts),
        out_shape=tuple(shape((rows, width), F32) for width in widths),
        in_specs=[HBM] * 6,
        out_specs=(HBM,) * 3,
        scratch_shapes=passage_scratch(widths, far, rows, wide),
        compiler_params=params,
        cost_estimate=cost(16 * rows * wide, 12 * rows * wide),
    )(place, returned, *p_parts, p_inverses)
    return (losses, *q_grads, *p_grads)


def solution(mesh):
    rows = P(AXES, None)
    return jax.shard_map(
        local,
        mesh=mesh,
        in_specs=(rows,) * 7 + (P(AXES),),
        out_specs=(P(AXES),) + (rows,) * 6,
        check_vma=False,
    )
```

```python
import functools
import math

import jax
import jax.numpy as jnp
from jax import lax
from jax.experimental import pallas as pl
from jax.experimental.pallas import tpu as pltpu
from jax.sharding import PartitionSpec as P

PROWS = 8
LANES = 128
AXES = ("dp", "group")

EPSILON = 1e-06
SHARPNESS = 20.0
EXP_SCALE = SHARPNESS * math.log2(math.e)
OFF = -1e30

F32 = jnp.float32
BF16 = jnp.bfloat16
HBM = pl.BlockSpec(memory_space=pltpu.HBM)
VMEM = pl.BlockSpec(memory_space=pltpu.VMEM)
SMEM = pl.BlockSpec(memory_space=pltpu.SMEM)
MIB = 1024 * 1024
NT = (((1,), (1,)), ((), ()))
TN = (((0,), (0,)), ((), ()))
NN = (((1,), (0,)), ((), ()))


def exchange(values):
    return lax.all_to_all(values, AXES, split_axis=0, concat_axis=0, tiled=True)


def cost(flops, moved):
    return pl.CostEstimate(flops=int(flops), bytes_accessed=int(moved), transcendentals=0)


def columns_of(widths):
    starts = {}
    at = 0
    for index in sorted(range(len(widths)), key=lambda i: -widths[i]):
        starts[index] = at
        at += widths[index]
    return [starts[i] for i in range(len(widths))]


def wanted_kernel(block_count, neg_ref, out_ref):
    peers = out_ref.shape[0]
    lists, entries = neg_ref.shape
    peer = lax.broadcasted_iota(jnp.int32, (peers, entries), 0)
    best = jnp.full((peers, entries), -1, jnp.int32)
    for row in range(lists):
        ids = jnp.broadcast_to(neg_ref[row : row + 1, :], (peers, entries))
        local_ids = ids - peer * block_count
        hit = (local_ids >= 0) & (local_ids < block_count)
        best = jnp.maximum(best, jnp.where(hit, local_ids, -1))
    best = jnp.max(best.astype(F32), axis=1, keepdims=True)
    out_ref[...] = jnp.broadcast_to(best, out_ref.shape).astype(jnp.int32)


def heads_kernel(widths, starts, raw0, raw1, raw2, after_ref, out_ref, inv_ref):
    del after_ref
    lane = lax.broadcasted_iota(jnp.int32, inv_ref.shape, 1)
    packed = jnp.zeros(inv_ref.shape, F32)
    for k, raw in enumerate((raw0, raw1, raw2)):
        values = raw[...].astype(F32)
        inverse = lax.rsqrt(jnp.sum(values * values, axis=1, keepdims=True) + EPSILON)
        out_ref[:, starts[k] : starts[k] + widths[k]] = (values * inverse).astype(BF16)
        packed = jnp.where(lane == k, inverse, packed)
    inv_ref[...] = packed


def gather_kernel(widths, starts, asked_ref, raw0, raw1, raw2, out_hbm, out_v, sems):
    raws = (raw0, raw1, raw2)
    pairs = out_v.shape[0] // 16
    parts = min(8, pairs)
    each = pairs // parts

    def block(raw, peer):
        ident = jnp.maximum(asked_ref[peer, 0], 0)
        start = pl.multiple_of((ident // 2) * 16, 16)
        both = raw[pl.ds(start, 16), :].astype(F32)
        return jnp.where(ident % 2 == 0, both[:8], both[8:])

    stores = []
    for part in range(parts):
        for pair in range(part * each, (part + 1) * each):
            for k in range(3):
                values = jnp.concatenate([block(raws[k], pair * 2), block(raws[k], pair * 2 + 1)], axis=0)
                inverse = lax.rsqrt(jnp.sum(values * values, axis=1, keepdims=True) + EPSILON)
                place = slice(starts[k], starts[k] + widths[k])
                out_v[pair * 16 : pair * 16 + 16, place] = (values * inverse).astype(BF16)
        here = pl.ds(part * each * 16, each * 16)
        store = pltpu.make_async_copy(out_v.at[here, :], out_hbm.at[here, :], sems.at[part])
        store.start()
        stores.append(store)
    for store in stores:
        store.wait()


def local_kernel(
    widths, starts, block_count, p_ref, q_ref, pos_ref, neg_ref,
    tot_ref, spos_ref, bias_ref, e_ref,
):
    rows = p_ref.shape[0]
    cols = pos_ref.shape[1]
    chunk = min(256, rows)
    pos = pos_ref[0:1, :]
    for k in range(3):
        span = slice(starts[k], starts[k] + widths[k])
        q = q_ref[:, span]
        tot = jnp.zeros((1, cols), F32)
        spos = jnp.zeros((1, cols), F32)
        for at in range(0, rows, chunk):
            s = lax.dot_general(p_ref[at : at + chunk, span], q, NT, preferred_element_type=F32)
            row = lax.broadcasted_iota(jnp.int32, (chunk, cols), 0) + at
            e = jnp.exp2(s * EXP_SCALE)
            e_ref[k, at : at + chunk, :] = e.astype(BF16)
            tot = tot + jnp.sum(e, axis=0, keepdims=True)
            spos = spos + jnp.sum(jnp.where(row == pos, s, 0.0), axis=0, keepdims=True)
        tot_ref[k : k + 1, :] = tot
        spos_ref[k : k + 1, :] = spos * SHARPNESS
    @pl.when(pl.program_id(0) == 0)
    def _():
        far = bias_ref.shape[0]
        lists, entries = neg_ref.shape
        peer = lax.broadcasted_iota(jnp.int32, (far, entries), 0) // PROWS
        lane = lax.broadcasted_iota(jnp.int32, bias_ref.shape, 1)
        bias = jnp.full(bias_ref.shape, OFF, F32)
        for b in range(lists):
            local_ids = jnp.broadcast_to(neg_ref[b : b + 1, :], (far, entries)) - peer * block_count
            hit = (local_ids >= 0) & (local_ids < block_count)
            listed = jnp.max(jnp.where(hit, 1.0, 0.0), axis=1, keepdims=True)
            bias = jnp.where((lane == b) & (listed > 0.0), 0.0, bias)
        bias_ref[...] = bias.astype(BF16)


def far_scratch(far, rows, wide):
    return [
        pltpu.VMEM((far, wide), BF16),
        pltpu.VMEM((rows, wide), BF16),
        pltpu.VMEM((far, LANES), BF16),
        pltpu.VMEM((8, rows), F32),
        pltpu.VMEM((8, rows), F32),
        pltpu.VMEM((8, rows), F32),
        pltpu.VMEM((8, rows), F32),
        pltpu.VMEM((3, far, rows), BF16),
        pltpu.VMEM((2, far, rows), F32),
        pltpu.VMEM((far, wide), BF16),
        pltpu.SemaphoreType.DMA((4, 3)),
        pltpu.SemaphoreType.DMA((4, 4)),
    ]


def far_kernel(
    widths, starts, lists, far_hbm, q_hbm, bias_hbm, tot_hbm, spos_hbm,
    term_hbm, scale_hbm, loss_hbm,
    far_ref, q_ref, bias_ref, tot_ref, spos_ref, scale_ref, loss_ref,
    g_ref, e_v, term_v, in_sems, out_sems,
):
    far, rows = g_ref.shape[1:]
    cols = rows // lists
    chunk = min(256, far)
    order = (0, 1, 2)
    loads = {}
    for k in order:
        span = pl.ds(starts[k], widths[k])
        loads[k] = [
            pltpu.make_async_copy(far_hbm.at[:, span], far_ref.at[:, span], in_sems.at[k, 0]),
            pltpu.make_async_copy(q_hbm.at[:, span], q_ref.at[:, span], in_sems.at[k, 1]),
        ]
        if k == order[0]:
            loads[k] += [
                pltpu.make_async_copy(bias_hbm, bias_ref, in_sems.at[3, 0]),
                pltpu.make_async_copy(tot_hbm, tot_ref, in_sems.at[3, 1]),
                pltpu.make_async_copy(spos_hbm, spos_ref, in_sems.at[3, 2]),
            ]
        for load in loads[k]:
            load.start()
    scale_ref[3:8, :] = jnp.zeros((5, rows), F32)
    loss_ref[3:8, :] = jnp.zeros((5, rows), F32)
    stores = []
    def scores(k):
        span = slice(starts[k], starts[k] + widths[k])
        for load in loads[k]:
            load.wait()
        for b in range(lists):
            at_q = slice(b * cols, (b + 1) * cols)
            q = q_ref[at_q, span]
            tot = tot_ref[k : k + 1, at_q]
            for at in range(0, far, chunk):
                s = lax.dot_general(far_ref[at : at + chunk, span], q, NT, preferred_element_type=F32)
                bias = bias_ref[at : at + chunk, :].astype(F32)[:, b : b + 1]
                e = jnp.exp2(s * EXP_SCALE + bias)
                tot = tot + jnp.sum(e, axis=0, keepdims=True)
                e_v[k % 2, at : at + chunk, at_q] = e
            scale = SHARPNESS / tot
            scale_ref[k : k + 1, at_q] = scale
            loss_ref[k : k + 1, at_q] = jnp.log(tot) - spos_ref[k : k + 1, at_q]
            for at in range(0, far, chunk):
                g_ref[k, at : at + chunk, at_q] = (e_v[k % 2, at : at + chunk, at_q] * scale).astype(BF16)

    def send(k):
        span = slice(starts[k], starts[k] + widths[k])
        for row in range(0, far, chunk):
            here = slice(row, row + chunk)
            part = jnp.concatenate(
                [
                    jnp.dot(g_ref[k, here, :], q_ref[:, at : at + 256], preferred_element_type=F32)
                    for at in range(starts[k], starts[k] + widths[k], 256)
                ],
                axis=1,
            )
            unit = far_ref[here, span].astype(F32)
            part = part - unit * jnp.sum(unit * part, axis=1, keepdims=True)
            term_v[here, span] = part.astype(BF16)
            place = (pl.ds(row, chunk), pl.ds(starts[k], widths[k]))
            store = pltpu.make_async_copy(
                term_v.at[place], term_hbm.at[place], out_sems.at[k, row // chunk]
            )
            store.start()
            stores.append(store)

    scores(order[0])
    send(order[0])
    scores(order[1])
    send(order[1])
    scores(order[2])
    for index, (ref, hbm) in enumerate(((scale_ref, scale_hbm), (loss_ref, loss_hbm))):
        stores.append(pltpu.make_async_copy(ref, hbm, out_sems.at[3, index]))
        stores[-1].start()
    send(order[2])
    for store in stores:
        store.wait()


def raw_gradient(raw, inverse, grad):
    unit = raw.astype(F32) * inverse
    return (grad - unit * jnp.sum(unit * grad, axis=1, keepdims=True)) * inverse


def near_kernel(
    k, lists, p_ref, q_ref, far_ref, e_ref, raw_ref, inv_ref, scale_ref, bias_ref, pos_ref,
    p_raw_ref, p_inv_ref, out_ref, part_ref, dp_v,
):
    rows = p_ref.shape[0]
    far = far_ref.shape[0]
    cols = q_ref.shape[0]
    q = q_ref[...]
    pos = pos_ref[0:1, :]
    scale = scale_ref[k : k + 1, :]
    chunk = min(256, rows, far)
    step = pl.program_id(0)
    lane = lax.broadcasted_iota(jnp.int32, (chunk, LANES), 1)
    parts = []
    for at in range(0, far, chunk):
        s = lax.dot_general(far_ref[at : at + chunk, :], q, NT, preferred_element_type=F32)
        bias = jnp.sum(jnp.where(lane == step, bias_ref[at : at + chunk, :].astype(F32), 0.0), axis=1, keepdims=True)
        parts.append((jnp.exp2(s * EXP_SCALE + bias) * scale).astype(BF16))
    dq = lax.dot_general(
        jnp.concatenate(parts, axis=0), far_ref[...], TN, preferred_element_type=F32
    )
    parts = []
    for at in range(0, rows, chunk):
        row = lax.broadcasted_iota(jnp.int32, (chunk, cols), 0) + at
        g = e_ref[0, at : at + chunk, :].astype(F32) * scale
        parts.append((g - jnp.where(row == pos, SHARPNESS, 0.0)).astype(BF16))
    weights = jnp.concatenate(parts, axis=0)
    dq = dq + lax.dot_general(weights, p_ref[...], TN, preferred_element_type=F32)
    dp = jnp.dot(weights, q, preferred_element_type=F32)

    @pl.when(step == 0)
    def _():
        dp_v[...] = dp

    @pl.when(step > 0)
    def _():
        dp_v[...] += dp

    out_ref[...] = raw_gradient(raw_ref[...], inv_ref[:, k : k + 1], dq)

    @pl.when(step == lists - 1)
    def _():
        for at in range(0, rows, chunk):
            here = slice(at, at + chunk)
            part = raw_gradient(p_raw_ref[here, :], p_inv_ref[here, k : k + 1], dp_v[here, :])
            part_ref[here, :] = part.astype(BF16)


def passage_scratch(widths, far, rows, wide):
    return (
        [
            pltpu.VMEM((far, wide), BF16),
            pltpu.VMEM((rows, far), BF16),
            pltpu.VMEM((rows, LANES), F32),
            pltpu.VMEM((1, far), jnp.int32),
        ]
        + [pltpu.VMEM((rows, width), BF16) for width in widths]
        + [pltpu.VMEM((rows, width), F32) for width in widths]
        + [pltpu.SemaphoreType.DMA((4, 3)), pltpu.SemaphoreType.DMA((3, 4))]
    )


def passage_kernel(
    widths, starts, place_hbm, term_hbm, part0, part1, part2, inv_hbm,
    out0, out1, out2,
    term_v, pick_v, inv_ref, place_ref, pv0, pv1, pv2, ov0, ov1, ov2, in_sems, out_sems,
):
    parts, outs = (part0, part1, part2), (out0, out1, out2)
    part_vs, out_vs = (pv0, pv1, pv2), (ov0, ov1, ov2)
    rows = ov0.shape[0]
    far = term_v.shape[0]
    order = (0, 1, 2)
    chunk = min(256, rows)
    small = (
        pltpu.make_async_copy(place_hbm, place_ref, in_sems.at[3, 0]),
        pltpu.make_async_copy(inv_hbm, inv_ref, in_sems.at[3, 1]),
    )
    for load in small:
        load.start()
    loads = {}
    for k in order:
        span = pl.ds(starts[k], widths[k])
        loads[k] = (
            pltpu.make_async_copy(term_hbm.at[:, span], term_v.at[:, span], in_sems.at[k, 0]),
            pltpu.make_async_copy(parts[k], part_vs[k], in_sems.at[k, 1]),
        )
        for load in loads[k]:
            load.start()
    for load in small:
        load.wait()
    place = place_ref[...]
    for at in range(0, rows, chunk):
        row = lax.broadcasted_iota(jnp.int32, (chunk, far), 0) + at
        pick_v[at : at + chunk, :] = jnp.where(row == place, 1.0, 0.0).astype(BF16)
    stores = []
    for k in order:
        for load in loads[k]:
            load.wait()
        terms = term_v[:, starts[k] : starts[k] + widths[k]]
        for at in range(0, rows, chunk):
            here = slice(at, at + chunk)
            inverse = inv_ref[here, k : k + 1]
            added = jnp.dot(pick_v[here, :], terms, preferred_element_type=F32)
            added = added * inverse
            out_vs[k][here, :] = part_vs[k][here, :].astype(F32) + added
            part = pl.ds(at, chunk)
            store = pltpu.make_async_copy(
                out_vs[k].at[part, :], outs[k].at[part, :], out_sems.at[k, at // chunk]
            )
            store.start()
            stores.append(store)
    for store in stores:
        store.wait()


def local(
    query_first, query_second, query_third,
    passage_first, passage_second, passage_third,
    neg_blocks, positives,
):
    devices = lax.axis_size(AXES)
    own = lax.axis_index(AXES)
    queries = (query_first, query_second, query_third)
    passages = (passage_first, passage_second, passage_third)
    widths = [values.shape[1] for values in queries]
    starts = columns_of(widths)
    wide = sum(widths)
    rows = query_first.shape[0]
    block_count = rows // PROWS
    lists, entries = neg_blocks.shape
    far = devices * PROWS
    cols = rows // lists
    params = pltpu.CompilerParams(vmem_limit_bytes=62 * MIB)
    shape = jax.ShapeDtypeStruct

    wanted = pl.pallas_call(
        functools.partial(wanted_kernel, block_count),
        out_shape=jax.ShapeDtypeStruct((devices, LANES), jnp.int32),
        in_specs=[VMEM],
        out_specs=VMEM,
        compiler_params=params,
    )(neg_blocks)
    asked = exchange(wanted[:, None, :]).reshape(devices, LANES)

    step = rows // 4
    row_block = lambda width: pl.BlockSpec((step, width), lambda i: (i, 0))

    def heads(values, after):
        return pl.pallas_call(
            functools.partial(heads_kernel, widths, starts),
            grid=(4,),
            out_shape=(shape((rows, wide), BF16), shape((rows, LANES), F32)),
            in_specs=[row_block(width) for width in widths] + [HBM],
            out_specs=(row_block(wide), row_block(LANES)),
            compiler_params=params,
            cost_estimate=cost(rows * wide * 4, rows * wide * 4),
        )(*values, after)

    send = pl.pallas_call(
        functools.partial(gather_kernel, widths, starts),
        out_shape=shape((far, wide), BF16),
        in_specs=[SMEM, VMEM, VMEM, VMEM],
        out_specs=HBM,
        scratch_shapes=[pltpu.VMEM((far, wide), BF16), pltpu.SemaphoreType.DMA((8,))],
        compiler_params=pltpu.CompilerParams(vmem_limit_bytes=62 * MIB),
        cost_estimate=cost(far * wide * 4, far * wide * 4),
    )(asked, *passages)
    fetched = exchange(send.reshape(devices, PROWS, wide)).reshape(far, wide)

    p_all, p_inverses = heads(passages, send)
    q_all, q_inverses = heads(queries, send)
    local_pos = (positives - own * rows).reshape(1, rows)
    whole = lambda dims: pl.BlockSpec(dims, lambda i: (0,) * len(dims))
    pos_block = pl.BlockSpec((1, cols), lambda i: (0, i))
    lane_block = pl.BlockSpec((8, cols), lambda i: (0, i))
    totals, positive_scores, bias, local_exps = pl.pallas_call(
        functools.partial(local_kernel, widths, starts, block_count),
        grid=(lists,),
        out_shape=(
            shape((8, rows), F32),
            shape((8, rows), F32),
            shape((far, LANES), BF16),
            shape((3, rows, rows), BF16),
        ),
        in_specs=[
            whole((rows, wide)),
            pl.BlockSpec((cols, wide), lambda i: (i, 0)),
            pos_block,
            whole((lists, entries)),
        ],
        out_specs=(
            lane_block,
            lane_block,
            whole((far, LANES)),
            pl.BlockSpec((3, rows, cols), lambda i: (0, 0, i)),
        ),
        compiler_params=params,
        cost_estimate=cost(2 * rows * rows * wide, rows * wide * 4),
    )(p_all, q_all, local_pos, neg_blocks)

    terms, scales, loss_rows = pl.pallas_call(
        functools.partial(far_kernel, widths, starts, lists),
        out_shape=(shape((far, wide), BF16), shape((8, rows), F32), shape((8, rows), F32)),
        in_specs=[HBM] * 5,
        out_specs=(HBM,) * 3,
        scratch_shapes=far_scratch(far, rows, wide),
        compiler_params=params,
        cost_estimate=cost(4 * far * rows * wide, 6 * far * wide),
    )(fetched, q_all, bias, totals, positive_scores)
    losses = loss_rows[0] + loss_rows[1] + loss_rows[2]
    returned = exchange(terms.reshape(devices, PROWS, wide)).reshape(far, wide)

    q_grads = []
    p_parts = []
    for k in range(3):
        width = widths[k]
        place = starts[k] // width
        q_grad, p_part = pl.pallas_call(
            functools.partial(near_kernel, k, lists),
            grid=(lists,),
            out_shape=(shape((rows, width), F32), shape((rows, width), BF16)),
            in_specs=[
                pl.BlockSpec((rows, width), lambda i, place=place: (0, place)),
                pl.BlockSpec((cols, width), lambda i, place=place: (i, place)),
                pl.BlockSpec((far, width), lambda i, place=place: (0, place)),
                pl.BlockSpec((1, rows, cols), lambda i, k=k: (k, 0, i)),
                pl.BlockSpec((cols, width), lambda i: (i, 0)),
                pl.BlockSpec((cols, LANES), lambda i: (i, 0)),
                lane_block,
                whole((far, LANES)),
                pos_block,
                whole((rows, width)),
                whole((rows, LANES)),
            ],
            out_specs=(pl.BlockSpec((cols, width), lambda i: (i, 0)), whole((rows, width))),
            scratch_shapes=[pltpu.VMEM((rows, width), F32)],
            compiler_params=params,
            cost_estimate=cost(8 * rows * rows * width, 16 * rows * width),
        )(
            p_all, q_all, fetched, local_exps, queries[k], q_inverses, scales, bias, local_pos,
            passages[k], p_inverses,
        )
        q_grads.append(q_grad)
        p_parts.append(p_part)

    offsets = jnp.arange(PROWS, dtype=jnp.int32)
    asked_ids = asked[:, :1]
    place = jnp.where(asked_ids >= 0, asked_ids * PROWS + offsets[None, :], -1).reshape(1, far)
    p_grads = pl.pallas_call(
        functools.partial(passage_kernel, widths, starts),
        out_shape=tuple(shape((rows, width), F32) for width in widths),
        in_specs=[HBM] * 6,
        out_specs=(HBM,) * 3,
        scratch_shapes=passage_scratch(widths, far, rows, wide),
        compiler_params=params,
        cost_estimate=cost(16 * rows * wide, 12 * rows * wide),
    )(place, returned, *p_parts, p_inverses)
    return (losses, *q_grads, *p_grads)


def solution(mesh):
    rows = P(AXES, None)
    return jax.shard_map(
        local,
        mesh=mesh,
        in_specs=(rows,) * 7 + (P(AXES),),
        out_specs=(P(AXES),) + (rows,) * 6,
        check_vma=False,
    )
```
